32 devices in a mesh: slab: 2 (over y), dom: 16 (over z, x, core).
Axes of the slice: x: 2, y: 2, z: 4, core: 2. Of those that a mesh axis runs over, the one named last changes fastest.
Arguments:
- state: bfloat16 [16, 64, 3072], P('dom', 'slab'), may hold values from -6 to 6
- send_index: int32 [16, 2, 16, 4], P('dom', 'slab'), may hold values from 0 to 47
- send_count: int32 [16, 2, 16], P('dom', 'slab'), may hold values from 1 to 4, as said below
- slot_target: int32 [16, 2, 64], P('dom', 'slab'), may hold values from 0 to 63
- cross_mass: bfloat16 [16, 2, 64, 4096], P('dom', 'slab'), may hold values from -0.75 to 0.75
- mass: float32 [16, 128, 4096], P('dom', 'slab'), as said below
- new_order: int32 [16, 2, 64], P('dom', 'slab'), may hold values from 0 to 63, each once within a row
Outputs:
- remapped: float32 [16, 128, 3072], P('dom', 'slab')
The draws below stay inside these ranges and needn't reach their ends.
Inputs may be any that keep to these rules, and one draw needn't show every extreme that they name: `send_count`: each sender has exactly 4 live slots to at least one peer. Every mass block is symmetric, and each diagonal entry is positive and exceeds the sum of magnitudes of the rest of its row.
All inputs are finite; a program needn't handle non-finite values.
Results may differ from the reference program's by a relative error of at most 0.0003.
Values may be sent and summed in bfloat16 or wider, within the bound.
A program may use at most 64 MiB of HBM per device.

```python
import jax
import jax.numpy as jnp
from jax import lax

Q = 64
V = 48
E_DEV = 32
NEW_DEV = 64
CAP = 4
ITERS = 3
RIM = 8
POOL = 48
DOMS = 16
SLABS = 2
GROUP = 4
N_SLAB = 2
N_DOM = 16


def draw_send_count(key, part):
    first = jax.random.fold_in(key, 11)
    second = jax.random.fold_in(key, 12)
    counts = jax.random.randint(first, (DOMS, SLABS, DOMS), 1, CAP + 1)
    where_full = jax.random.randint(second, (DOMS, SLABS, 1), 0, DOMS)
    column = jnp.arange(DOMS)[None, None, :]
    return jnp.where(column == where_full, CAP, counts).astype(jnp.int32)


def draw_mass(key, part):
    first = jax.random.fold_in(key, 21)
    second = jax.random.fold_in(key, 22)
    third = jax.random.fold_in(key, 23)
    rows = SLABS * NEW_DEV
    raw = jax.random.uniform(first, (DOMS, rows, Q, Q), jnp.float32, -0.015, 0.015)
    sym = 0.5 * (raw + jnp.swapaxes(raw, 2, 3))
    diag = jax.random.uniform(second, (DOMS, rows, Q), jnp.float32, 1.0, 2.0)
    eye = jnp.eye(Q, dtype=jnp.float32)
    blocks = sym * (1.0 - eye) + diag[..., None] * eye
    logs = jax.random.uniform(third, (DOMS, rows, 1, 1), jnp.float32, 0.0, 2.3)
    position = jnp.arange(DOMS, dtype=jnp.float32)[:, None, None, None] / max(DOMS - 1, 1)
    blocks = blocks * jnp.exp(logs) * (1.0 + 2.0 * position)
    return blocks.reshape(DOMS, rows, Q * Q)


def plant(drawn, rng, least, largest):
    shape = drawn.shape
    index_at = [jax.random.randint(jax.random.fold_in(rng, axis), (), 0, shape[axis]) for axis in range(len(shape))]
    drawn = drawn.at[tuple(index_at)].set(least)
    longest = shape.index(max(shape))
    index_at[longest] = (index_at[longest] + 1) % shape[longest]
    return drawn.at[tuple(index_at)].set(largest)


def block_scale(rng, extent, pieces, low, top_value):
    gain = 1.0
    for axis_at, parts in pieces:
        draws = jax.random.uniform(jax.random.fold_in(jax.random.fold_in(rng, 6), axis_at), (parts,), jnp.float32, low / len(pieces), top_value / len(pieces))
        gain = gain * jnp.repeat(jnp.exp(draws), extent[axis_at] // parts).reshape((-1,) + (1,) * (len(extent) - 1 - axis_at))
    return gain


def normal_values(stream_key, shape, scale, limit, cuts=(), held_as=jnp.bfloat16):
    result = jax.random.normal(stream_key, shape, jnp.float32) * scale
    if len(cuts) > 0:
        result = block_scale(stream_key, shape, cuts, -0.22, 0.18) * result
    return jnp.clip(result, min=-limit, max=limit).astype(held_as)


def setup_inputs(seed: int = 0) -> dict:
    key_of = jax.random.split(jax.random.key(seed), 8)
    return {
        "state": normal_values(key_of[0], (DOMS, SLABS * E_DEV, V * Q), 1.0, 6.0, ((0, 16), (1, 2))),
        "send_index": plant(jax.random.randint(key_of[1], (DOMS, SLABS, DOMS, CAP), 0, POOL), jax.random.fold_in(key_of[1], 1), 0, POOL - 1).astype(jnp.int32),
        "send_count": draw_send_count(jax.random.fold_in(key_of[7], 71), 0),
        "slot_target": plant(jax.random.randint(key_of[3], (DOMS, SLABS, DOMS * CAP), 0, NEW_DEV), jax.random.fold_in(key_of[3], 1), 0, NEW_DEV - 1).astype(jnp.int32),
        "cross_mass": normal_values(key_of[4], (DOMS, SLABS, DOMS * CAP, Q * Q), Q ** -0.5, 0.75, ((0, 16), (1, 2))),
        "mass": draw_mass(jax.random.fold_in(key_of[7], 71), 0),
        "new_order": jax.vmap(lambda own: jax.random.permutation(own, NEW_DEV))(jax.random.split(key_of[6], DOMS * SLABS)).reshape((DOMS, SLABS, NEW_DEV)).astype(jnp.int32),
    }


def reference(state, send_index, send_count, slot_target, cross_mass, mass, new_order):
    extended = jnp.pad(state, ((0, 0), (RIM, RIM), (0, 0)))
    pools = jnp.stack([extended[:, s * E_DEV:s * E_DEV + POOL] for s in range(N_SLAB)], axis=1)
    live = jnp.arange(CAP)[None, None, None, :] < send_count[..., None]

    def receive(k):
        picks = lax.dynamic_index_in_dim(send_index, k, 2, False)
        packets = jnp.take_along_axis(pools, picks[..., None], axis=2)
        alive = lax.dynamic_index_in_dim(live, k, 2, False)
        packets = jnp.where(alive[..., None], packets, jnp.zeros_like(packets))
        packets = jnp.transpose(packets, (1, 0, 2, 3)).reshape(N_SLAB, N_DOM * CAP, V, Q).astype(jnp.float32)
        blocks = cross_mass[k].reshape(N_SLAB, N_DOM * CAP, Q, Q).astype(jnp.float32)
        contrib = jnp.einsum('sjqp,sjvp->sjvq', blocks, packets, precision=lax.Precision.HIGHEST)
        onehot = (slot_target[k][..., None] == jnp.arange(NEW_DEV)[None, None, :]).astype(jnp.float32)
        return jnp.einsum('sjn,sjx->snx', onehot, contrib.reshape(N_SLAB, N_DOM * CAP, V * Q), precision=lax.Precision.HIGHEST)

    rhs = lax.map(receive, jnp.arange(N_DOM)).reshape(N_DOM, N_SLAB, NEW_DEV, V, Q)
    blocks = mass.reshape(N_DOM, N_SLAB, NEW_DEV, Q, Q)

    def apply_mass(field):
        return jnp.einsum('ksnqp,ksnvp->ksnvq', blocks, field, precision=lax.Precision.HIGHEST)

    def inner(left, right):
        return jnp.sum(left * right, axis=(0, 1, 2, 4))[:, None]

    solution = jnp.zeros_like(rhs)
    residual = rhs
    direction = rhs
    norm_now = inner(residual, residual)
    for step in range(ITERS):
        image = apply_mass(direction)
        alpha = norm_now / inner(direction, image)
        solution = solution + alpha * direction
        residual = residual - alpha * image
        norm_next = inner(residual, residual)
        direction = residual + (norm_next / norm_now) * direction
        norm_now = norm_next
    flat = solution.reshape(N_DOM, N_SLAB, NEW_DEV, V * Q)
    ordered = jnp.take_along_axis(flat, new_order[..., None], axis=2)
    ordered = ordered.reshape(N_DOM, N_SLAB, N_DOM, GROUP, V * Q)
    ordered = jnp.transpose(ordered, (2, 1, 0, 3, 4))
    return ordered.reshape(N_DOM, N_SLAB * NEW_DEV, V * Q)
```

```python
import functools

import jax
import jax.numpy as jnp
from jax import lax
from jax.experimental import pallas as pl
from jax.experimental.pallas import tpu as pltpu
from jax.sharding import PartitionSpec as P

Q = 64
V = 48
RIM = 8
LANES = 128
HALF = V // 2
ITERS = 3
F32 = jnp.float32
BF16 = jnp.bfloat16
LIMIT = 32767.0


def at(index, unit):
    return pl.multiple_of(index * unit, unit)


def left_half(shape):
    return lax.broadcasted_iota(jnp.int32, shape, 1) < Q


def swap(value):
    return pltpu.roll(value, Q, 1)


def interleave(first, second):
    left = left_half(first.shape)
    return jnp.where(left, first, swap(second)), jnp.where(left, swap(first), second)


def split(value):
    high = value.astype(BF16)
    return high, (value - high.astype(F32)).astype(BF16)


def eye(rows):
    shape = (rows, LANES)
    return lax.broadcasted_iota(jnp.int32, shape, 0) == lax.broadcasted_iota(jnp.int32, shape, 1)


def column_to_row(column):
    spread = jnp.where(eye(column.shape[0]), column, 0.0)
    return jnp.sum(spread, axis=0, keepdims=True)


def row_to_column(row, rows):
    spread = jnp.where(eye(rows), row, 0.0)
    return jnp.sum(spread, axis=1, keepdims=True)


def pair_blocks(source, group, block):
    left = left_half((8, LANES))

    def body(t, carry):
        both = source[pl.ds(at(group, 16), 16), pl.ds(at(t, LANES), LANES)].astype(F32)
        first, second = both[:8], both[8:]
        block[pl.ds(2 * t, 8, stride=LANES), :] = jnp.where(left, first, 0.0)
        block[pl.ds(2 * t + 1, 8, stride=LANES), :] = jnp.where(left, swap(first), 0.0)
        block[pl.ds(Q + 2 * t, 8, stride=LANES), :] = jnp.where(left, 0.0, swap(second))
        block[pl.ds(Q + 2 * t + 1, 8, stride=LANES), :] = jnp.where(left, 0.0, second)
        return carry

    lax.fori_loop(0, Q // 2, body, 0, unroll=8)


def kernel(
    slabs, doms, cap, group,
    index_ref, count_ref, order_ref, target_ref, state_ref, cross_ref, mass_ref,
    out_ref,
    pool, up_out, down_out, up_in, down_in, packets, received, block, cross, blocks,
    contrib, residual, direction, image, answer, element, codes, codes_in, scales, scales_in,
    placed, sums, sums_in,
    halo_send, halo_recv, packet_send, packet_recv, sum_send, sum_recv,
    code_send, code_recv, scale_send, scale_recv,
):
    my_slab, my_dom = lax.axis_index("slab"), lax.axis_index("dom")
    devices = slabs * doms
    me = my_slab * doms + my_dom
    elements = state_ref.shape[0]
    slots = cross_ref.shape[0]
    new_count = mass_ref.shape[0]
    chunk = cap * HALF
    code_rows = codes.shape[0] // doms

    def device(i):
        there = lax.rem(me + i, devices)
        return {"slab": lax.div(there, doms), "dom": lax.rem(there, doms)}

    barrier = pltpu.get_barrier_semaphore()

    def greet(i, carry):
        pl.semaphore_signal(barrier, inc=1, device_id=device(i), device_id_type=pl.DeviceIdType.MESH)
        return carry

    lax.fori_loop(1, devices, greet, 0)

    def unfold(t, carry):
        for row in range(0, elements, 16):
            part = state_ref[row:row + 16, pl.ds(at(t, LANES), LANES)].astype(F32)
            pool[pl.ds((RIM + row) * HALF + t, 8, stride=HALF), :] = part[:8]
            pool[pl.ds((RIM + row + 8) * HALF + t, 8, stride=HALF), :] = part[8:]
        return carry

    lax.fori_loop(0, HALF, unfold, 0, unroll=4)
    rim_rows = RIM * HALF
    last = (RIM + elements) * HALF
    down_out[...] = pool[rim_rows:2 * rim_rows, :].astype(BF16)
    up_out[...] = pool[last - rim_rows:last, :].astype(BF16)
    pl.semaphore_wait(barrier, devices - 1)

    def halo(which, src, dst, slab):
        return pltpu.make_async_remote_copy(
            src_ref=src, dst_ref=dst, send_sem=halo_send.at[which], recv_sem=halo_recv.at[which],
            device_id={"slab": slab, "dom": my_dom}, device_id_type=pl.DeviceIdType.MESH,
        )

    up = halo(0, up_out, up_in, lax.rem(my_slab + 1, slabs))
    down = halo(1, down_out, down_in, lax.rem(my_slab + slabs - 1, slabs))

    @pl.when(my_slab < slabs - 1)
    def _():
        up.start()

    @pl.when(my_slab > 0)
    def _():
        down.start()

    def prepare_mass(j, carry):
        pair_blocks(mass_ref, j, block)

        def cut(i, inner):
            high, low = split(block[pl.ds(at(i, LANES), LANES), :])
            blocks[pl.ds(at(j * 8 + i, LANES), LANES), 0:LANES] = high
            blocks[pl.ds(at(j * 8 + i, LANES), LANES), LANES:2 * LANES] = low
            return inner

        return lax.fori_loop(0, 8, cut, carry)

    lax.fori_loop(0, new_count // 32, prepare_mass, 0)

    @pl.when(my_slab > 0)
    def _():
        up.wait_recv()
        pool[0:rim_rows, :] = up_in[...].astype(F32)

    @pl.when(my_slab == 0)
    def _():
        pool[0:rim_rows, :] = jnp.zeros((rim_rows, LANES), F32)

    @pl.when(my_slab < slabs - 1)
    def _():
        down.wait_recv()
        pool[last:last + rim_rows, :] = down_in[...].astype(F32)

    @pl.when(my_slab == slabs - 1)
    def _():
        pool[last:last + rim_rows, :] = jnp.zeros((rim_rows, LANES), F32)

    def pick(dom):
        live = count_ref[0, dom]
        rows = []
        for c in range(cap):
            row = pool[pl.ds(index_ref[dom, c] * HALF, HALF), :]
            rows.append(row * jnp.minimum(jnp.maximum(live - c, 0), 1).astype(F32))
        return jnp.concatenate(rows, axis=0).astype(BF16)

    def packet(dom):
        return pltpu.make_async_remote_copy(
            src_ref=packets.at[pl.ds(at(dom, chunk), chunk), :],
            dst_ref=received.at[pl.ds(at(my_dom, chunk), chunk), :],
            send_sem=packet_send.at[dom], recv_sem=packet_recv.at[my_dom],
            device_id={"slab": my_slab, "dom": dom}, device_id_type=pl.DeviceIdType.MESH,
        )

    def send_packet(i, carry):
        dom = lax.rem(my_dom + i, doms)
        packets[pl.ds(at(dom, chunk), chunk), :] = pick(dom)
        packet(dom).start()
        return carry

    lax.fori_loop(1, doms, send_packet, 0)
    received[pl.ds(at(my_dom, chunk), chunk), :] = pick(my_dom)

    lax.fori_loop(new_count // 32, new_count // 16, prepare_mass, 0)

    def prepare_cross(j, carry):
        pair_blocks(cross_ref, j, block)

        def cut(i, inner):
            cross[pl.ds(at(j * 8 + i, LANES), LANES), :] = block[pl.ds(at(i, LANES), LANES), :].astype(BF16)
            return inner

        return lax.fori_loop(0, 8, cut, carry)

    lax.fori_loop(0, slots // 16, prepare_cross, 0)

    def arrive(dom, carry):
        @pl.when(dom != my_dom)
        def _():
            pltpu.make_async_remote_copy(
                src_ref=packets.at[pl.ds(at(dom, chunk), chunk), :],
                dst_ref=received.at[pl.ds(at(dom, chunk), chunk), :],
                send_sem=packet_send.at[dom], recv_sem=packet_recv.at[dom],
                device_id={"slab": my_slab, "dom": dom}, device_id_type=pl.DeviceIdType.MESH,
            ).wait()

        return carry

    lax.fori_loop(0, doms, arrive, 0)

    senders = 16 // cap

    def product(step, carry):
        j, h = lax.div(step, senders // 2), lax.rem(step, senders // 2)
        first = received[pl.ds(at(j * senders + h, chunk), chunk), :].astype(F32)
        second = received[pl.ds(at(j * senders + senders // 2 + h, chunk), chunk), :].astype(F32)
        for c in range(cap):
            part = slice(c * HALF, (c + 1) * HALF)
            pair = j * 8 + h * cap + c
            field = jnp.concatenate(interleave(first[part], second[part]), axis=0).astype(BF16)
            matrix = cross[pl.ds(at(pair, LANES), LANES), :]
            contrib[pl.ds(at(pair, V), V), :] = lax.dot_general(
                field, matrix, (((1,), (1,)), ((), ())), preferred_element_type=F32
            )
        return carry

    lax.fori_loop(0, doms // 2, product, 0)

    shape = (new_count, slots)
    onehot = jnp.where(lax.broadcasted_iota(jnp.int32, shape, 0) == target_ref[...], 1.0, 0.0).astype(BF16)
    pairs_in = slots // 2

    def scatter(t, carry):
        even = contrib[pl.ds(t, pairs_in, stride=V), :]
        odd = contrib[pl.ds(HALF + t, pairs_in, stride=V), :]
        first, second = interleave(even, odd)
        rows = []
        for j in range(pairs_in // 8):
            rows += [first[j * 8:j * 8 + 8], second[j * 8:j * 8 + 8]]
        terms = jnp.concatenate(split(jnp.concatenate(rows, axis=0)), axis=1)
        total = jnp.dot(onehot, terms, preferred_element_type=F32)
        total = total[:, :LANES] + total[:, LANES:]
        for j in range(new_count // 16):
            even, odd = interleave(total[j * 16:j * 16 + 8], total[j * 16 + 8:j * 16 + 16])
            residual[pl.ds(j * 8 * V + t, 8, stride=V), :] = even
            residual[pl.ds(j * 8 * V + HALF + t, 8, stride=V), :] = odd
        return carry

    lax.fori_loop(0, HALF, scatter, 0, unroll=2)

    pairs = new_count // 2

    def apply_mass(pair, field):
        terms = jnp.concatenate(split(field), axis=0)
        result = jnp.dot(terms, blocks[pl.ds(at(pair, LANES), LANES), :], preferred_element_type=F32)
        return (result[V:, :LANES] + result[:V, LANES:]) + result[:V, :LANES]

    def all_sum(step, left, right):
        own = column_to_row(jnp.sum(jnp.concatenate([left, right], axis=0), axis=1, keepdims=True))
        sums[step:step + 1, :] = own

        def send(i, carry):
            pltpu.make_async_remote_copy(
                src_ref=sums.at[step:step + 1, :],
                dst_ref=sums_in.at[step, pl.ds(i - 1, 1), :],
                send_sem=sum_send.at[step, i - 1], recv_sem=sum_recv.at[step, i - 1],
                device_id=device(i), device_id_type=pl.DeviceIdType.MESH,
            ).start()
            return carry

        def wait(i, carry):
            pltpu.make_async_remote_copy(
                src_ref=sums.at[step:step + 1, :],
                dst_ref=sums_in.at[step, pl.ds(i - 1, 1), :],
                send_sem=sum_send.at[step, i - 1], recv_sem=sum_recv.at[step, i - 1],
                device_id=device(i), device_id_type=pl.DeviceIdType.MESH,
            ).wait()
            return carry

        lax.fori_loop(1, devices, send, 0)
        lax.fori_loop(1, devices, wait, 0)
        total = own + jnp.sum(sums_in[step, 0:devices - 1, :], axis=0, keepdims=True)
        column = row_to_column(total, 2 * V)
        return column[:V], column[V:]

    zero = jnp.zeros((V, LANES), F32)

    def first_pass(pair, carry):
        rr, rw = carry
        at_pair = pl.ds(at(pair, V), V)
        r = residual[at_pair, :]
        w = apply_mass(pair, r)
        image[at_pair, :] = w
        return rr + r * r, rw + r * w

    rr, rw = all_sum(0, *lax.fori_loop(0, pairs, first_pass, (zero, zero), unroll=2))
    alpha = rr / rw

    def second_pass(pair, carry):
        nn, nw = carry
        at_pair = pl.ds(at(pair, V), V)
        p = residual[at_pair, :]
        r = p - alpha * image[at_pair, :]
        direction[at_pair, :] = p
        answer[at_pair, :] = alpha * p
        residual[at_pair, :] = r
        w = apply_mass(pair, r)
        contrib_w[at_pair, :] = w
        return nn + r * r, nw + r * w

    contrib_w = element
    nn, nw = all_sum(1, *lax.fori_loop(0, pairs, second_pass, (zero, zero), unroll=2))
    beta = nn / rr
    alpha = nn / (nw - beta * nn / alpha)
    rr = nn

    def third_pass(pair, carry):
        nn, nw = carry
        at_pair = pl.ds(at(pair, V), V)
        r = residual[at_pair, :]
        p = r + beta * direction[at_pair, :]
        s = contrib_w[at_pair, :] + beta * image[at_pair, :]
        direction[at_pair, :] = p
        answer[at_pair, :] = answer[at_pair, :] + alpha * p
        r = r - alpha * s
        residual[at_pair, :] = r
        w = apply_mass(pair, r)
        return nn + r * r, nw + r * w

    nn, nw = all_sum(2, *lax.fori_loop(0, pairs, third_pass, (zero, zero), unroll=2))
    beta = nn / rr
    alpha = nn / (nw - beta * nn / alpha)

    def last_pass(pair, carry):
        at_pair = pl.ds(at(pair, V), V)
        p = residual[at_pair, :] + beta * direction[at_pair, :]
        x = answer[at_pair, :] + alpha * p
        first, second = interleave(x[:HALF], x[HALF:])
        number = lax.div(pair, 8) * 16 + lax.rem(pair, 8)
        element[pl.ds(at(number, HALF), HALF), :] = first
        element[pl.ds(at(number + 8, HALF), HALF), :] = second
        return carry

    lax.fori_loop(0, pairs, last_pass, 0, unroll=2)

    used = group * HALF

    def code(dom):
        rows = [
            element[pl.ds(order_ref[0, dom * group + g] * HALF, HALF), :] for g in range(group)
        ]
        value = jnp.concatenate(rows, axis=0)
        top = jnp.maximum(jnp.max(jnp.abs(value), axis=1, keepdims=True), 1e-30)
        coded = jnp.round(value * (LIMIT / top)).astype(jnp.int32)
        if code_rows > used:
            coded = jnp.concatenate([coded, jnp.zeros((code_rows - used, LANES), jnp.int32)], axis=0)
        return coded.astype(jnp.int16), column_to_row(top * (1.0 / LIMIT))

    def code_copies(to, frm, dst):
        where = {"slab": my_slab, "dom": to}
        return [
            pltpu.make_async_remote_copy(
                src_ref=codes.at[pl.ds(at(to, code_rows), code_rows), :],
                dst_ref=codes_in.at[pl.ds(at(dst, code_rows), code_rows), :],
                send_sem=code_send.at[to], recv_sem=code_recv.at[frm],
                device_id=where, device_id_type=pl.DeviceIdType.MESH,
            ),
            pltpu.make_async_remote_copy(
                src_ref=scales.at[pl.ds(to, 1), :], dst_ref=scales_in.at[pl.ds(dst, 1), :],
                send_sem=scale_send.at[to], recv_sem=scale_recv.at[frm],
                device_id=where, device_id_type=pl.DeviceIdType.MESH,
            ),
        ]

    def send_code(i, carry):
        dom = lax.rem(my_dom + i, doms)
        coded, scale = code(dom)
        codes[pl.ds(at(dom, code_rows), code_rows), :] = coded
        scales[pl.ds(dom, 1), :] = scale
        for copy in code_copies(dom, my_dom, my_dom):
            copy.start()
        return carry

    lax.fori_loop(1, doms, send_code, 0)
    coded, scale = code(my_dom)
    codes_in[pl.ds(at(my_dom, code_rows), code_rows), :] = coded
    scales_in[pl.ds(my_dom, 1), :] = scale

    def place(dom, carry):
        @pl.when(dom != my_dom)
        def _():
            for copy in code_copies(dom, dom, dom):
                copy.wait()

        value = codes_in[pl.ds(at(dom, code_rows), code_rows), :].astype(jnp.int32).astype(F32)[:used]
        scale = row_to_column(scales_in[pl.ds(dom, 1), :], used)
        placed[pl.ds(at(dom, used), used), :] = value * scale
        return carry

    lax.fori_loop(0, doms, place, 0)

    def fold(t, carry):
        for row in range(0, new_count, 8):
            out_ref[row:row + 8, pl.ds(at(t, LANES), LANES)] = placed[pl.ds(row * HALF + t, 8, stride=HALF), :]
        return carry

    lax.fori_loop(0, HALF, fold, 0, unroll=2)

    @pl.when(my_slab < slabs - 1)
    def _():
        up.wait_send()

    @pl.when(my_slab > 0)
    def _():
        down.wait_send()


def per_device(slabs, doms, state, send_index, send_count, slot_target, cross_mass, mass, new_order):
    cap = send_index.shape[3]
    new_count = mass.shape[1]
    group = new_count // doms
    slots = doms * cap
    pool_rows = (state.shape[1] + 2 * RIM) * HALF
    rim_rows = RIM * HALF
    code_rows = -(-group * HALF // 16) * 16
    devices = slabs * doms
    steps = ITERS
    vmem, smem = pltpu.VMEM, pltpu.SMEM
    dma = pltpu.SemaphoreType.DMA
    field = vmem((new_count * HALF, LANES), F32)
    scratch = [
        vmem((pool_rows, LANES), F32),
        *[vmem((rim_rows, LANES), BF16)] * 4,
        vmem((slots * HALF, LANES), BF16),
        vmem((slots * HALF, LANES), BF16),
        vmem((8 * LANES, LANES), F32),
        vmem((slots // 2 * LANES, LANES), BF16),
        vmem((new_count // 2 * LANES, 2 * LANES), BF16),
        vmem((slots * HALF, LANES), F32),
        *[field] * 5,
        vmem((doms * code_rows, LANES), jnp.int16),
        vmem((doms * code_rows, LANES), jnp.int16),
        vmem((doms, LANES), F32),
        vmem((doms, LANES), F32),
        field,
        vmem((8, LANES), F32),
        vmem((steps, devices, LANES), F32),
        dma((2,)), dma((2,)), dma((doms,)), dma((doms,)),
        dma((steps, devices)), dma((steps, devices)),
        dma((doms,)), dma((doms,)), dma((doms,)), dma((doms,)),
    ]
    out = pl.pallas_call(
        functools.partial(kernel, slabs, doms, cap, group),
        out_shape=jax.ShapeDtypeStruct((new_count, V * Q), F32),
        in_specs=[pl.BlockSpec(memory_space=smem)] * 3 + [pl.BlockSpec(memory_space=vmem)] * 4,
        out_specs=pl.BlockSpec(memory_space=vmem),
        scratch_shapes=scratch,
        compiler_params=pltpu.CompilerParams(
            collective_id=0, has_side_effects=True, vmem_limit_bytes=48 * 1024 * 1024
        ),
        cost_estimate=pl.CostEstimate(flops=10**9, bytes_accessed=4 * 10**6, transcendentals=0),
    )(
        send_index[0, 0], send_count[0], new_order[0], slot_target[0],
        state[0], cross_mass[0, 0], mass[0],
    )
    return out[None]


def solution(mesh):
    in_specs = (
        P("dom", "slab", None),
        P("dom", "slab", None, None),
        P("dom", "slab", None),
        P("dom", "slab", None),
        P("dom", "slab", None, None),
        P("dom", "slab", None),
        P("dom", "slab", None),
    )
    return jax.shard_map(
        functools.partial(per_device, mesh.shape["slab"], mesh.shape["dom"]),
        mesh=mesh, in_specs=in_specs, out_specs=P("dom", "slab", None), check_vma=False,
    )
```

```python
import functools

import jax
import jax.numpy as jnp
from jax import lax
from jax.experimental import pallas as pl
from jax.experimental.pallas import tpu as pltpu
from jax.sharding import PartitionSpec as P

Q = 64
V = 48
RIM = 8
LANES = 128
HALF = V // 2
ITERS = 3
F32 = jnp.float32
BF16 = jnp.bfloat16
LIMIT = 32767.0


def at(index, unit):
    return pl.multiple_of(index * unit, unit)


def left_half(shape):
    return lax.broadcasted_iota(jnp.int32, shape, 1) < Q


def swap(value):
    return pltpu.roll(value, Q, 1)


def interleave(first, second):
    left = left_half(first.shape)
    return jnp.where(left, first, swap(second)), jnp.where(left, swap(first), second)


def split(value):
    high = value.astype(BF16)
    return high, (value - high.astype(F32)).astype(BF16)


def eye(rows):
    shape = (rows, LANES)
    return lax.broadcasted_iota(jnp.int32, shape, 0) == lax.broadcasted_iota(jnp.int32, shape, 1)


def column_to_row(column):
    spread = jnp.where(eye(column.shape[0]), column, 0.0)
    return jnp.sum(spread, axis=0, keepdims=True)


def row_to_column(row, rows):
    spread = jnp.where(eye(rows), row, 0.0)
    return jnp.sum(spread, axis=1, keepdims=True)


def pair_blocks(source, group, block):
    left = left_half((8, LANES))

    def body(t, carry):
        both = source[pl.ds(at(group, 16), 16), pl.ds(at(t, LANES), LANES)].astype(F32)
        first, second = both[:8], both[8:]
        block[pl.ds(2 * t, 8, stride=LANES), :] = jnp.where(left, first, 0.0)
        block[pl.ds(2 * t + 1, 8, stride=LANES), :] = jnp.where(left, swap(first), 0.0)
        block[pl.ds(Q + 2 * t, 8, stride=LANES), :] = jnp.where(left, 0.0, swap(second))
        block[pl.ds(Q + 2 * t + 1, 8, stride=LANES), :] = jnp.where(left, 0.0, second)
        return carry

    lax.fori_loop(0, Q // 2, body, 0, unroll=8)


def kernel(
    slabs, doms, cap, group,
    index_ref, count_ref, order_ref, target_ref, state_hbm, cross_hbm, mass_hbm,
    out_ref,
    state_ref, cross_ref, mass_ref, load_sem,
    pool, up_out, down_out, up_in, down_in, packets, received, block, cross, blocks,
    contrib, residual, direction, image, answer, element, codes, codes_in, scales, scales_in,
    placed, sums, sums_in,
    halo_send, halo_recv, packet_send, packet_recv, sum_send, sum_recv,
    code_send, code_recv, scale_send, scale_recv,
):
    my_slab, my_dom = lax.axis_index("slab"), lax.axis_index("dom")
    devices = slabs * doms
    me = my_slab * doms + my_dom
    elements = state_ref.shape[0]
    slots = cross_ref.shape[0]
    new_count = mass_ref.shape[0]
    chunk = cap * HALF
    code_rows = codes.shape[0] // doms

    def device(i):
        there = lax.rem(me + i, devices)
        return {"slab": lax.div(there, doms), "dom": lax.rem(there, doms)}

    loads = [
        pltpu.make_async_copy(src, dst, load_sem.at[n])
        for n, (src, dst) in enumerate(
            ((state_hbm, state_ref), (mass_hbm, mass_ref), (cross_hbm, cross_ref))
        )
    ]
    for load in loads:
        load.start()
    barrier = pltpu.get_barrier_semaphore()

    def greet(i, carry):
        pl.semaphore_signal(barrier, inc=1, device_id=device(i), device_id_type=pl.DeviceIdType.MESH)
        return carry

    lax.fori_loop(1, devices, greet, 0)

    loads[0].wait()

    def unfold(t, carry):
        for row in range(0, elements, 16):
            part = state_ref[row:row + 16, pl.ds(at(t, LANES), LANES)].astype(F32)
            pool[pl.ds((RIM + row) * HALF + t, 8, stride=HALF), :] = part[:8]
            pool[pl.ds((RIM + row + 8) * HALF + t, 8, stride=HALF), :] = part[8:]
        return carry

    lax.fori_loop(0, HALF, unfold, 0, unroll=4)
    rim_rows = RIM * HALF
    last = (RIM + elements) * HALF
    down_out[...] = pool[rim_rows:2 * rim_rows, :].astype(BF16)
    up_out[...] = pool[last - rim_rows:last, :].astype(BF16)
    pl.semaphore_wait(barrier, devices - 1)

    def halo(which, src, dst, slab):
        return pltpu.make_async_remote_copy(
            src_ref=src, dst_ref=dst, send_sem=halo_send.at[which], recv_sem=halo_recv.at[which],
            device_id={"slab": slab, "dom": my_dom}, device_id_type=pl.DeviceIdType.MESH,
        )

    up = halo(0, up_out, up_in, lax.rem(my_slab + 1, slabs))
    down = halo(1, down_out, down_in, lax.rem(my_slab + slabs - 1, slabs))

    @pl.when(my_slab < slabs - 1)
    def _():
        up.start()

    @pl.when(my_slab > 0)
    def _():
        down.start()

    loads[1].wait()

    def prepare_mass(j, carry):
        pair_blocks(mass_ref, j, block)

        def cut(i, inner):
            high, low = split(block[pl.ds(at(i, LANES), LANES), :])
            blocks[pl.ds(at(j * 8 + i, LANES), LANES), 0:LANES] = high
            blocks[pl.ds(at(j * 8 + i, LANES), LANES), LANES:2 * LANES] = low
            return inner

        return lax.fori_loop(0, 8, cut, carry, unroll=4)

    lax.fori_loop(0, new_count // 32, prepare_mass, 0)

    @pl.when(my_slab > 0)
    def _():
        up.wait_recv()
        pool[0:rim_rows, :] = up_in[...].astype(F32)

    @pl.when(my_slab == 0)
    def _():
        pool[0:rim_rows, :] = jnp.zeros((rim_rows, LANES), F32)

    @pl.when(my_slab < slabs - 1)
    def _():
        down.wait_recv()
        pool[last:last + rim_rows, :] = down_in[...].astype(F32)

    @pl.when(my_slab == slabs - 1)
    def _():
        pool[last:last + rim_rows, :] = jnp.zeros((rim_rows, LANES), F32)

    def pick(dom):
        live = count_ref[0, dom]
        rows = []
        for c in range(cap):
            row = pool[pl.ds(index_ref[c, dom] * HALF, HALF), :]
            rows.append(row * jnp.minimum(jnp.maximum(live - c, 0), 1).astype(F32))
        return jnp.concatenate(rows, axis=0).astype(BF16)

    def packet(dom):
        return pltpu.make_async_remote_copy(
            src_ref=packets.at[pl.ds(at(dom, chunk), chunk), :],
            dst_ref=received.at[pl.ds(at(my_dom, chunk), chunk), :],
            send_sem=packet_send.at[dom], recv_sem=packet_recv.at[my_dom],
            device_id={"slab": my_slab, "dom": dom}, device_id_type=pl.DeviceIdType.MESH,
        )

    def partner(i):
        return lax.rem(my_dom + 1 + lax.rem(i + doms // 2 - 2, doms - 1), doms)

    def send_packet(i, carry):
        dom = partner(i)
        packets[pl.ds(at(dom, chunk), chunk), :] = pick(dom)
        packet(dom).start()
        return carry

    lax.fori_loop(1, doms, send_packet, 0)
    received[pl.ds(at(my_dom, chunk), chunk), :] = pick(my_dom)

    lax.fori_loop(new_count // 32, new_count // 16, prepare_mass, 0)

    def prepare_cross(j, carry):
        pair_blocks(cross_ref, j, block)

        def cut(i, inner):
            cross[pl.ds(at(j * 8 + i, LANES), LANES), :] = jnp.transpose(
                block[pl.ds(at(i, LANES), LANES), :]
            ).astype(BF16)
            return inner

        return lax.fori_loop(0, 8, cut, carry, unroll=4)

    loads[2].wait()
    lax.fori_loop(0, slots // 16, prepare_cross, 0)

    def arrive(dom, carry):
        @pl.when(dom != my_dom)
        def _():
            pltpu.make_async_remote_copy(
                src_ref=packets.at[pl.ds(at(dom, chunk), chunk), :],
                dst_ref=received.at[pl.ds(at(dom, chunk), chunk), :],
                send_sem=packet_send.at[dom], recv_sem=packet_recv.at[dom],
                device_id={"slab": my_slab, "dom": dom}, device_id_type=pl.DeviceIdType.MESH,
            ).wait()

        return carry

    lax.fori_loop(0, doms, arrive, 0)

    senders = 16 // cap

    def product(step, carry):
        j, h = lax.div(step, senders // 2), lax.rem(step, senders // 2)
        first = received[pl.ds(at(j * senders + h, chunk), chunk), :].astype(F32)
        second = received[pl.ds(at(j * senders + senders // 2 + h, chunk), chunk), :].astype(F32)
        for c in range(cap):
            part = slice(c * HALF, (c + 1) * HALF)
            pair = j * 8 + h * cap + c
            field = jnp.concatenate(interleave(first[part], second[part]), axis=0).astype(BF16)
            matrix = cross[pl.ds(at(pair, LANES), LANES), :]
            contrib[pl.ds(at(pair, V), V), :] = jnp.dot(
                field, matrix, preferred_element_type=F32
            )
        return carry

    lax.fori_loop(0, doms // 2, product, 0, unroll=2)

    shape = (new_count, slots)
    onehot = jnp.where(lax.broadcasted_iota(jnp.int32, shape, 0) == target_ref[...], 1.0, 0.0).astype(BF16)
    pairs_in = slots // 2

    def scatter(t, carry):
        even = contrib[pl.ds(t, pairs_in, stride=V), :]
        odd = contrib[pl.ds(HALF + t, pairs_in, stride=V), :]
        first, second = interleave(even, odd)
        rows = []
        for j in range(pairs_in // 8):
            rows += [first[j * 8:j * 8 + 8], second[j * 8:j * 8 + 8]]
        terms = jnp.concatenate(split(jnp.concatenate(rows, axis=0)), axis=1)
        total = jnp.dot(onehot, terms, preferred_element_type=F32)
        total = total[:, :LANES] + total[:, LANES:]
        for j in range(new_count // 16):
            even, odd = interleave(total[j * 16:j * 16 + 8], total[j * 16 + 8:j * 16 + 16])
            residual[pl.ds(j * 8 * V + t, 8, stride=V), :] = even
            residual[pl.ds(j * 8 * V + HALF + t, 8, stride=V), :] = odd
        return carry

    lax.fori_loop(0, HALF, scatter, 0, unroll=6)

    pairs = new_count // 2

    def apply_mass(pair, field):
        terms = jnp.concatenate(split(field), axis=0)
        result = jnp.dot(terms, blocks[pl.ds(at(pair, LANES), LANES), :], preferred_element_type=F32)
        return (result[V:, :LANES] + result[:V, LANES:]) + result[:V, :LANES]

    def all_sum(step, left, right):
        own = column_to_row(jnp.sum(jnp.concatenate([left, right], axis=0), axis=1, keepdims=True))
        sums[step:step + 1, :] = own

        def send(i, carry):
            pltpu.make_async_remote_copy(
                src_ref=sums.at[step:step + 1, :],
                dst_ref=sums_in.at[step, pl.ds(i - 1, 1), :],
                send_sem=sum_send.at[step], recv_sem=sum_recv.at[step],
                device_id=device(i), device_id_type=pl.DeviceIdType.MESH,
            ).start()
            return carry

        lax.fori_loop(1, devices, send, 0)
        arrived = sums_in.at[step, 0:devices - 1, :]
        pltpu.make_async_copy(arrived, arrived, sum_recv.at[step]).wait()
        total = own + jnp.sum(sums_in[step, 0:devices - 1, :], axis=0, keepdims=True)
        column = row_to_column(total, 2 * V)
        return column[:V], column[V:]

    zero = jnp.zeros((V, LANES), F32)

    def first_pass(pair, carry):
        rr, rw = carry
        at_pair = pl.ds(at(pair, V), V)
        r = residual[at_pair, :]
        w = apply_mass(pair, r)
        image[at_pair, :] = w
        return rr + r * r, rw + r * w

    rr, rw = all_sum(0, *lax.fori_loop(0, pairs, first_pass, (zero, zero), unroll=8))
    alpha = rr / rw

    def second_pass(pair, carry):
        nn, nw = carry
        at_pair = pl.ds(at(pair, V), V)
        p = residual[at_pair, :]
        r = p - alpha * image[at_pair, :]
        direction[at_pair, :] = p
        answer[at_pair, :] = alpha * p
        residual[at_pair, :] = r
        w = apply_mass(pair, r)
        contrib_w[at_pair, :] = w
        return nn + r * r, nw + r * w

    contrib_w = element
    nn, nw = all_sum(1, *lax.fori_loop(0, pairs, second_pass, (zero, zero), unroll=8))
    beta = nn / rr
    alpha = nn / (nw - beta * nn / alpha)
    rr = nn

    def third_pass(pair, carry):
        nn, nw = carry
        at_pair = pl.ds(at(pair, V), V)
        r = residual[at_pair, :]
        p = r + beta * direction[at_pair, :]
        s = contrib_w[at_pair, :] + beta * image[at_pair, :]
        direction[at_pair, :] = p
        answer[at_pair, :] = answer[at_pair, :] + alpha * p
        r = r - alpha * s
        residual[at_pair, :] = r
        w = apply_mass(pair, r)
        return nn + r * r, nw + r * w

    nn, nw = all_sum(2, *lax.fori_loop(0, pairs, third_pass, (zero, zero), unroll=8))
    beta = nn / rr
    alpha = nn / (nw - beta * nn / alpha)

    def last_pass(pair, carry):
        at_pair = pl.ds(at(pair, V), V)
        p = residual[at_pair, :] + beta * direction[at_pair, :]
        x = answer[at_pair, :] + alpha * p
        first, second = interleave(x[:HALF], x[HALF:])
        number = lax.div(pair, 8) * 16 + lax.rem(pair, 8)
        element[pl.ds(at(number, HALF), HALF), :] = first
        element[pl.ds(at(number + 8, HALF), HALF), :] = second
        return carry

    lax.fori_loop(0, pairs, last_pass, 0, unroll=4)

    used = group * HALF

    def code(dom):
        rows = [
            element[pl.ds(order_ref[0, dom * group + g] * HALF, HALF), :] for g in range(group)
        ]
        value = jnp.concatenate(rows, axis=0)
        top = jnp.maximum(jnp.max(jnp.abs(value), axis=1, keepdims=True), 1e-30)
        coded = jnp.round(value * (LIMIT / top)).astype(jnp.int32)
        if code_rows > used:
            coded = jnp.concatenate([coded, jnp.zeros((code_rows - used, LANES), jnp.int32)], axis=0)
        return coded.astype(jnp.int16), column_to_row(top * (1.0 / LIMIT))

    def code_copies(to, frm, dst):
        where = {"slab": my_slab, "dom": to}
        return [
            pltpu.make_async_remote_copy(
                src_ref=codes.at[pl.ds(at(to, code_rows), code_rows), :],
                dst_ref=codes_in.at[pl.ds(at(dst, code_rows), code_rows), :],
                send_sem=code_send.at[to], recv_sem=code_recv.at[frm],
                device_id=where, device_id_type=pl.DeviceIdType.MESH,
            ),
            pltpu.make_async_remote_copy(
                src_ref=scales.at[pl.ds(to, 1), :], dst_ref=scales_in.at[pl.ds(dst, 1), :],
                send_sem=scale_send.at[to], recv_sem=scale_recv.at[frm],
                device_id=where, device_id_type=pl.DeviceIdType.MESH,
            ),
        ]

    def send_code(i, carry):
        dom = partner(i)
        coded, scale = code(dom)
        codes[pl.ds(at(dom, code_rows), code_rows), :] = coded
        scales[pl.ds(dom, 1), :] = scale
        for copy in code_copies(dom, my_dom, my_dom):
            copy.start()
        return carry

    lax.fori_loop(1, doms, send_code, 0)
    coded, scale = code(my_dom)
    codes_in[pl.ds(at(my_dom, code_rows), code_rows), :] = coded
    scales_in[pl.ds(my_dom, 1), :] = scale

    def place(dom, carry):
        @pl.when(dom != my_dom)
        def _():
            for copy in code_copies(dom, dom, dom):
                copy.wait()

        value = codes_in[pl.ds(at(dom, code_rows), code_rows), :].astype(jnp.int32).astype(F32)[:used]
        scale = row_to_column(scales_in[pl.ds(dom, 1), :], used)
        placed[pl.ds(at(dom, used), used), :] = value * scale
        return carry

    lax.fori_loop(0, doms, place, 0)

    def fold(t, carry):
        for row in range(0, new_count, 8):
            out_ref[row:row + 8, pl.ds(at(t, LANES), LANES)] = placed[pl.ds(row * HALF + t, 8, stride=HALF), :]
        return carry

    lax.fori_loop(0, HALF, fold, 0, unroll=2)

    for step in range(ITERS):
        left = sums_in.at[step, 0:devices - 1, :]
        pltpu.make_async_copy(left, left, sum_send.at[step]).wait()

    @pl.when(my_slab < slabs - 1)
    def _():
        up.wait_send()

    @pl.when(my_slab > 0)
    def _():
        down.wait_send()


def per_device(slabs, doms, state, send_index, send_count, slot_target, cross_mass, mass, new_order):
    cap = send_index.shape[3]
    new_count = mass.shape[1]
    group = new_count // doms
    slots = doms * cap
    pool_rows = (state.shape[1] + 2 * RIM) * HALF
    rim_rows = RIM * HALF
    code_rows = -(-group * HALF // 16) * 16
    devices = slabs * doms
    steps = ITERS
    vmem, smem = pltpu.VMEM, pltpu.SMEM
    dma = pltpu.SemaphoreType.DMA
    field = vmem((new_count * HALF, LANES), F32)
    scratch = [
        vmem(state.shape[1:], BF16),
        vmem((slots, Q * Q), BF16),
        vmem((new_count, Q * Q), F32),
        dma((3,)),
        vmem((pool_rows, LANES), F32),
        *[vmem((rim_rows, LANES), BF16)] * 4,
        vmem((slots * HALF, LANES), BF16),
        vmem((slots * HALF, LANES), BF16),
        vmem((8 * LANES, LANES), F32),
        vmem((slots // 2 * LANES, LANES), BF16),
        vmem((new_count // 2 * LANES, 2 * LANES), BF16),
        vmem((slots * HALF, LANES), F32),
        *[field] * 5,
        vmem((doms * code_rows, LANES), jnp.int16),
        vmem((doms * code_rows, LANES), jnp.int16),
        vmem((doms, LANES), F32),
        vmem((doms, LANES), F32),
        field,
        vmem((8, LANES), F32),
        vmem((steps, devices, LANES), F32),
        dma((2,)), dma((2,)), dma((doms,)), dma((doms,)),
        dma((steps,)), dma((steps,)),
        dma((doms,)), dma((doms,)), dma((doms,)), dma((doms,)),
    ]
    out = pl.pallas_call(
        functools.partial(kernel, slabs, doms, cap, group),
        out_shape=jax.ShapeDtypeStruct((new_count, V * Q), F32),
        in_specs=[pl.BlockSpec(memory_space=smem)] * 3 + [pl.BlockSpec(memory_space=vmem)]
        + [pl.BlockSpec(memory_space=pltpu.HBM)] * 3,
        out_specs=pl.BlockSpec(memory_space=vmem),
        scratch_shapes=scratch,
        compiler_params=pltpu.CompilerParams(
            collective_id=0, has_side_effects=True, vmem_limit_bytes=48 * 1024 * 1024
        ),
        cost_estimate=pl.CostEstimate(flops=10**9, bytes_accessed=4 * 10**6, transcendentals=0),
    )(
        send_index[0, 0].T, send_count[0], new_order[0], slot_target[0],
        state[0], cross_mass[0, 0], mass[0],
    )
    return out[None]


def solution(mesh):
    in_specs = (
        P("dom", "slab", None),
        P("dom", "slab", None, None),
        P("dom", "slab", None),
        P("dom", "slab", None),
        P("dom", "slab", None, None),
        P("dom", "slab", None),
        P("dom", "slab", None),
    )
    return jax.shard_map(
        functools.partial(per_device, mesh.shape["slab"], mesh.shape["dom"]),
        mesh=mesh, in_specs=in_specs, out_specs=P("dom", "slab", None), check_vma=False,
    )
```

```python
import functools

import jax
import jax.numpy as jnp
from jax import lax
from jax.experimental import pallas as pl
from jax.experimental.pallas import tpu as pltpu
from jax.sharding import PartitionSpec as P

Q = 64
V = 48
RIM = 8
LANES = 128
HALF = V // 2
ITERS = 3
F32 = jnp.float32
BF16 = jnp.bfloat16
LIMIT = 32767.0


def at(index, unit):
    return pl.multiple_of(index * unit, unit)


def left_half(shape):
    return lax.broadcasted_iota(jnp.int32, shape, 1) < Q


def swap(value):
    return pltpu.roll(value, Q, 1)


def interleave(first, second):
    left = left_half(first.shape)
    return jnp.where(left, first, swap(second)), jnp.where(left, swap(first), second)


def split(value):
    high = value.astype(BF16)
    return high, (value - high.astype(F32)).astype(BF16)


def eye(rows):
    shape = (rows, LANES)
    return lax.broadcasted_iota(jnp.int32, shape, 0) == lax.broadcasted_iota(jnp.int32, shape, 1)


def column_to_row(column):
    spread = jnp.where(eye(column.shape[0]), column, 0.0)
    return jnp.sum(spread, axis=0, keepdims=True)


def row_to_column(row, rows):
    spread = jnp.where(eye(rows), row, 0.0)
    return jnp.sum(spread, axis=1, keepdims=True)


def pair_blocks(source, group, block):
    left = left_half((8, LANES))

    def body(t, carry):
        both = source[pl.ds(at(group, 16), 16), pl.ds(at(t, LANES), LANES)].astype(F32)
        first, second = both[:8], both[8:]
        block[pl.ds(2 * t, 8, stride=LANES), :] = jnp.where(left, first, 0.0)
        block[pl.ds(2 * t + 1, 8, stride=LANES), :] = jnp.where(left, swap(first), 0.0)
        block[pl.ds(Q + 2 * t, 8, stride=LANES), :] = jnp.where(left, 0.0, swap(second))
        block[pl.ds(Q + 2 * t + 1, 8, stride=LANES), :] = jnp.where(left, 0.0, second)
        return carry

    lax.fori_loop(0, Q // 2, body, 0, unroll=8)


def kernel(
    slabs, doms, cap, group,
    index_ref, count_ref, order_ref, target_ref, state_hbm, cross_hbm, mass_hbm,
    out_ref,
    state_ref, cross_ref, mass_ref, load_sem,
    pool, up_out, down_out, up_in, down_in, packets, received, block, cross, blocks,
    contrib, residual, image, z_ref, next_residual, next_image, flat_x, flat_p, flat_r, codes, codes_in, scales, scales_in,
    placed, sums, sums_in,
    halo_send, halo_recv, packet_send, packet_recv, sum_send, sum_recv,
    code_send, code_recv, scale_send, scale_recv,
):
    my_slab, my_dom = lax.axis_index("slab"), lax.axis_index("dom")
    devices = slabs * doms
    me = my_slab * doms + my_dom
    elements = state_ref.shape[0]
    slots = cross_ref.shape[0]
    new_count = mass_ref.shape[0]
    chunk = cap * HALF
    code_rows = codes.shape[0] // doms

    def device(i):
        there = lax.rem(me + i, devices)
        return {"slab": lax.div(there, doms), "dom": lax.rem(there, doms)}

    loads = [
        pltpu.make_async_copy(src, dst, load_sem.at[n])
        for n, (src, dst) in enumerate(
            ((state_hbm, state_ref), (mass_hbm, mass_ref), (cross_hbm, cross_ref))
        )
    ]
    for load in loads:
        load.start()
    barrier = pltpu.get_barrier_semaphore()

    def greet(i, carry):
        pl.semaphore_signal(barrier, inc=1, device_id=device(i), device_id_type=pl.DeviceIdType.MESH)
        return carry

    lax.fori_loop(1, devices, greet, 0)

    loads[0].wait()

    def unfold(t, carry):
        for row in range(0, elements, 16):
            part = state_ref[row:row + 16, pl.ds(at(t, LANES), LANES)].astype(F32)
            pool[pl.ds((RIM + row) * HALF + t, 8, stride=HALF), :] = part[:8]
            pool[pl.ds((RIM + row + 8) * HALF + t, 8, stride=HALF), :] = part[8:]
        return carry

    lax.fori_loop(0, HALF, unfold, 0, unroll=4)
    rim_rows = RIM * HALF
    last = (RIM + elements) * HALF
    down_out[...] = pool[rim_rows:2 * rim_rows, :].astype(BF16)
    up_out[...] = pool[last - rim_rows:last, :].astype(BF16)
    pl.semaphore_wait(barrier, devices - 1)

    def halo(which, src, dst, slab):
        return pltpu.make_async_remote_copy(
            src_ref=src, dst_ref=dst, send_sem=halo_send.at[which], recv_sem=halo_recv.at[which],
            device_id={"slab": slab, "dom": my_dom}, device_id_type=pl.DeviceIdType.MESH,
        )

    up = halo(0, up_out, up_in, lax.rem(my_slab + 1, slabs))
    down = halo(1, down_out, down_in, lax.rem(my_slab + slabs - 1, slabs))

    @pl.when(my_slab < slabs - 1)
    def _():
        up.start()

    @pl.when(my_slab > 0)
    def _():
        down.start()

    loads[1].wait()

    def prepare_mass(j, carry):
        pair_blocks(mass_ref, j, block)

        def cut(i, inner):
            high, low = split(block[pl.ds(at(i, LANES), LANES), :])
            blocks[pl.ds(at(j * 8 + i, LANES), LANES), 0:LANES] = high
            blocks[pl.ds(at(j * 8 + i, LANES), LANES), LANES:2 * LANES] = low
            return inner

        return lax.fori_loop(0, 8, cut, carry, unroll=4)

    lax.fori_loop(0, new_count // 32, prepare_mass, 0)

    @pl.when(my_slab > 0)
    def _():
        up.wait_recv()
        pool[0:rim_rows, :] = up_in[...].astype(F32)

    @pl.when(my_slab == 0)
    def _():
        pool[0:rim_rows, :] = jnp.zeros((rim_rows, LANES), F32)

    @pl.when(my_slab < slabs - 1)
    def _():
        down.wait_recv()
        pool[last:last + rim_rows, :] = down_in[...].astype(F32)

    @pl.when(my_slab == slabs - 1)
    def _():
        pool[last:last + rim_rows, :] = jnp.zeros((rim_rows, LANES), F32)

    def pick(dom):
        live = count_ref[0, dom]
        rows = []
        for c in range(cap):
            row = pool[pl.ds(index_ref[c, dom] * HALF, HALF), :]
            rows.append(row * jnp.minimum(jnp.maximum(live - c, 0), 1).astype(F32))
        return jnp.concatenate(rows, axis=0).astype(BF16)

    def packet(dom):
        return pltpu.make_async_remote_copy(
            src_ref=packets.at[pl.ds(at(dom, chunk), chunk), :],
            dst_ref=received.at[pl.ds(at(my_dom, chunk), chunk), :],
            send_sem=packet_send.at[dom], recv_sem=packet_recv.at[my_dom],
            device_id={"slab": my_slab, "dom": dom}, device_id_type=pl.DeviceIdType.MESH,
        )

    def partner(i):
        return lax.rem(my_dom + 1 + lax.rem(i + doms // 2 - 2, doms - 1), doms)

    def send_packet(i, carry):
        dom = partner(i)
        packets[pl.ds(at(dom, chunk), chunk), :] = pick(dom)
        packet(dom).start()
        return carry

    lax.fori_loop(1, doms, send_packet, 0)
    received[pl.ds(at(my_dom, chunk), chunk), :] = pick(my_dom)

    lax.fori_loop(new_count // 32, new_count // 16, prepare_mass, 0)

    def prepare_cross(j, carry):
        pair_blocks(cross_ref, j, block)

        def cut(i, inner):
            cross[pl.ds(at(j * 8 + i, LANES), LANES), :] = jnp.transpose(
                block[pl.ds(at(i, LANES), LANES), :]
            ).astype(BF16)
            return inner

        return lax.fori_loop(0, 8, cut, carry, unroll=4)

    loads[2].wait()
    lax.fori_loop(0, slots // 16, prepare_cross, 0)

    def arrive(dom, carry):
        @pl.when(dom != my_dom)
        def _():
            pltpu.make_async_remote_copy(
                src_ref=packets.at[pl.ds(at(dom, chunk), chunk), :],
                dst_ref=received.at[pl.ds(at(dom, chunk), chunk), :],
                send_sem=packet_send.at[dom], recv_sem=packet_recv.at[dom],
                device_id={"slab": my_slab, "dom": dom}, device_id_type=pl.DeviceIdType.MESH,
            ).wait()

        return carry

    lax.fori_loop(0, doms, arrive, 0)

    senders = 16 // cap

    def product(step, carry):
        j, h = lax.div(step, senders // 2), lax.rem(step, senders // 2)
        first = received[pl.ds(at(j * senders + h, chunk), chunk), :].astype(F32)
        second = received[pl.ds(at(j * senders + senders // 2 + h, chunk), chunk), :].astype(F32)
        for c in range(cap):
            part = slice(c * HALF, (c + 1) * HALF)
            pair = j * 8 + h * cap + c
            field = jnp.concatenate(interleave(first[part], second[part]), axis=0).astype(BF16)
            matrix = cross[pl.ds(at(pair, LANES), LANES), :]
            contrib[pl.ds(at(pair, V), V), :] = jnp.dot(
                field, matrix, preferred_element_type=F32
            )
        return carry

    lax.fori_loop(0, doms // 2, product, 0, unroll=4)

    shape = (new_count, slots)
    onehot = jnp.where(lax.broadcasted_iota(jnp.int32, shape, 0) == target_ref[...], 1.0, 0.0).astype(BF16)
    pairs_in = slots // 2

    def scatter(t, carry):
        even = contrib[pl.ds(t, pairs_in, stride=V), :]
        odd = contrib[pl.ds(HALF + t, pairs_in, stride=V), :]
        first, second = interleave(even, odd)
        rows = []
        for j in range(pairs_in // 8):
            rows += [first[j * 8:j * 8 + 8], second[j * 8:j * 8 + 8]]
        terms = jnp.concatenate(split(jnp.concatenate(rows, axis=0)), axis=1)
        total = jnp.dot(onehot, terms, preferred_element_type=F32)
        total = total[:, :LANES] + total[:, LANES:]
        for j in range(new_count // 16):
            even, odd = interleave(total[j * 16:j * 16 + 8], total[j * 16 + 8:j * 16 + 16])
            residual[pl.ds(j * 8 * V + t, 8, stride=V), :] = even
            residual[pl.ds(j * 8 * V + HALF + t, 8, stride=V), :] = odd
        return carry

    lax.fori_loop(0, HALF, scatter, 0, unroll=6)

    pairs = new_count // 2

    def apply_mass(pair, field):
        terms = jnp.concatenate(split(field), axis=0)
        result = jnp.dot(terms, blocks[pl.ds(at(pair, LANES), LANES), :], preferred_element_type=F32)
        return (result[V:, :LANES] + result[:V, LANES:]) + result[:V, :LANES]

    def sum_start(step, left, right):
        own = column_to_row(jnp.sum(jnp.concatenate([left, right], axis=0), axis=1, keepdims=True))
        sums[step:step + 1, :] = own

        def send(i, carry):
            pltpu.make_async_remote_copy(
                src_ref=sums.at[step:step + 1, :],
                dst_ref=sums_in.at[step, pl.ds(i - 1, 1), :],
                send_sem=sum_send.at[step], recv_sem=sum_recv.at[step],
                device_id=device(i), device_id_type=pl.DeviceIdType.MESH,
            ).start()
            return carry

        lax.fori_loop(1, devices, send, 0)
        return own

    def sum_end(step, own):
        arrived = sums_in.at[step, 0:devices - 1, :]
        pltpu.make_async_copy(arrived, arrived, sum_recv.at[step]).wait()
        total = own + jnp.sum(sums_in[step, 0:devices - 1, :], axis=0, keepdims=True)
        column = row_to_column(total, 2 * V)
        return column[:V], column[V:]

    zero = jnp.zeros((V, LANES), F32)

    def first_pass(pair, carry):
        rr, rw = carry
        at_pair = pl.ds(at(pair, V), V)
        r = residual[at_pair, :]
        w = apply_mass(pair, r)
        image[at_pair, :] = w
        return rr + r * r, rw + r * w

    own = sum_start(0, *lax.fori_loop(0, pairs, first_pass, (zero, zero), unroll=8))

    def image_of_image(pair, carry):
        at_pair = pl.ds(at(pair, V), V)
        z_ref[at_pair, :] = apply_mass(pair, image[at_pair, :])
        return carry

    lax.fori_loop(0, pairs, image_of_image, 0, unroll=8)
    rr, rw = sum_end(0, own)
    alpha = rr / rw

    def second_pass(pair, carry):
        nn, nw = carry
        at_pair = pl.ds(at(pair, V), V)
        s = image[at_pair, :]
        r = residual[at_pair, :] - alpha * s
        w = s - alpha * z_ref[at_pair, :]
        next_residual[at_pair, :] = r
        next_image[at_pair, :] = w
        return nn + r * r, nw + r * w

    own = sum_start(1, *lax.fori_loop(0, pairs, second_pass, (zero, zero), unroll=4))

    def next_image_of_image(pair, carry):
        at_pair = pl.ds(at(pair, V), V)
        contrib[at_pair, :] = apply_mass(pair, next_image[at_pair, :])
        return carry

    lax.fori_loop(0, pairs, next_image_of_image, 0, unroll=8)
    nn, nw = sum_end(1, own)
    first_alpha = alpha
    beta = nn / rr
    alpha = nn / (nw - beta * nn / alpha)
    rr = nn

    def third_pass(pair, carry):
        nn, nw = carry
        at_pair = pl.ds(at(pair, V), V)
        b = residual[at_pair, :]
        r = next_residual[at_pair, :]
        w = next_image[at_pair, :]
        p = r + beta * b
        s = w + beta * image[at_pair, :]
        z = contrib[at_pair, :] + beta * z_ref[at_pair, :]
        residual[at_pair, :] = first_alpha * b + alpha * p
        image[at_pair, :] = p
        r = r - alpha * s
        w = w - alpha * z
        next_residual[at_pair, :] = r
        return nn + r * r, nw + r * w

    own = sum_start(2, *lax.fori_loop(0, pairs, third_pass, (zero, zero), unroll=4))

    def flatten(pair, carry):
        at_pair = pl.ds(at(pair, V), V)
        number = lax.div(pair, 8) * 16 + lax.rem(pair, 8)
        for src, dst in ((residual, flat_x), (image, flat_p), (next_residual, flat_r)):
            value = src[at_pair, :]
            first, second = interleave(value[:HALF], value[HALF:])
            dst[pl.ds(at(number, HALF), HALF), :] = first
            dst[pl.ds(at(number + 8, HALF), HALF), :] = second
        return carry

    lax.fori_loop(0, pairs, flatten, 0, unroll=4)
    nn, nw = sum_end(2, own)
    beta = nn / rr
    alpha = nn / (nw - beta * nn / alpha)

    def flat_factor(column):
        wide = jnp.broadcast_to(column, (V, LANES))
        return jnp.where(left_half((HALF, LANES)), wide[:HALF], wide[HALF:])

    factor_r = flat_factor(alpha)
    factor_p = flat_factor(alpha * beta)

    used = group * HALF

    def code(dom):
        rows = []
        for g in range(group):
            which = pl.ds(order_ref[0, dom * group + g] * HALF, HALF)
            rows.append(flat_x[which, :] + (factor_p * flat_p[which, :] + factor_r * flat_r[which, :]))
        value = jnp.concatenate(rows, axis=0)
        top = jnp.maximum(jnp.max(jnp.abs(value), axis=1, keepdims=True), 1e-30)
        coded = jnp.round(value * (LIMIT / top)).astype(jnp.int32)
        if code_rows > used:
            coded = jnp.concatenate([coded, jnp.zeros((code_rows - used, LANES), jnp.int32)], axis=0)
        return coded.astype(jnp.int16), column_to_row(top * (1.0 / LIMIT))

    def code_copies(to, frm, dst):
        where = {"slab": my_slab, "dom": to}
        return [
            pltpu.make_async_remote_copy(
                src_ref=codes.at[pl.ds(at(to, code_rows), code_rows), :],
                dst_ref=codes_in.at[pl.ds(at(dst, code_rows), code_rows), :],
                send_sem=code_send.at[to], recv_sem=code_recv.at[frm],
                device_id=where, device_id_type=pl.DeviceIdType.MESH,
            ),
            pltpu.make_async_remote_copy(
                src_ref=scales.at[pl.ds(to, 1), :], dst_ref=scales_in.at[pl.ds(dst, 1), :],
                send_sem=scale_send.at[to], recv_sem=scale_recv.at[frm],
                device_id=where, device_id_type=pl.DeviceIdType.MESH,
            ),
        ]

    def send_code(i, carry):
        dom = partner(i)
        coded, scale = code(dom)
        codes[pl.ds(at(dom, code_rows), code_rows), :] = coded
        scales[pl.ds(dom, 1), :] = scale
        for copy in code_copies(dom, my_dom, my_dom):
            copy.start()
        return carry

    lax.fori_loop(1, doms, send_code, 0)
    coded, scale = code(my_dom)
    codes_in[pl.ds(at(my_dom, code_rows), code_rows), :] = coded
    scales_in[pl.ds(my_dom, 1), :] = scale

    def place(rows, carry):
        for n in range(8 // group):
            dom = rows * (8 // group) + n

            @pl.when(dom != my_dom)
            def _():
                for copy in code_copies(dom, dom, dom):
                    copy.wait()

            value = codes_in[pl.ds(at(dom, code_rows), code_rows), :].astype(jnp.int32).astype(F32)[:used]
            scale = row_to_column(scales_in[pl.ds(dom, 1), :], used)
            placed[n * used:(n + 1) * used, :] = value * scale
        for t in range(HALF):
            out_ref[pl.ds(at(rows, 8), 8), t * LANES:(t + 1) * LANES] = placed[pl.ds(t, 8, stride=HALF), :]
        return carry

    lax.fori_loop(0, new_count // 8, place, 0)

    for step in range(ITERS):
        left = sums_in.at[step, 0:devices - 1, :]
        pltpu.make_async_copy(left, left, sum_send.at[step]).wait()

    @pl.when(my_slab < slabs - 1)
    def _():
        up.wait_send()

    @pl.when(my_slab > 0)
    def _():
        down.wait_send()


def per_device(slabs, doms, state, send_index, send_count, slot_target, cross_mass, mass, new_order):
    cap = send_index.shape[3]
    new_count = mass.shape[1]
    group = new_count // doms
    slots = doms * cap
    pool_rows = (state.shape[1] + 2 * RIM) * HALF
    rim_rows = RIM * HALF
    code_rows = -(-group * HALF // 16) * 16
    devices = slabs * doms
    steps = ITERS
    vmem, smem = pltpu.VMEM, pltpu.SMEM
    dma = pltpu.SemaphoreType.DMA
    field = vmem((new_count * HALF, LANES), F32)
    scratch = [
        vmem(state.shape[1:], BF16),
        vmem((slots, Q * Q), BF16),
        vmem((new_count, Q * Q), F32),
        dma((3,)),
        vmem((pool_rows, LANES), F32),
        *[vmem((rim_rows, LANES), BF16)] * 4,
        vmem((slots * HALF, LANES), BF16),
        vmem((slots * HALF, LANES), BF16),
        vmem((8 * LANES, LANES), F32),
        vmem((slots // 2 * LANES, LANES), BF16),
        vmem((new_count // 2 * LANES, 2 * LANES), BF16),
        vmem((max(slots, new_count) * HALF, LANES), F32),
        *[field] * 8,
        vmem((doms * code_rows, LANES), jnp.int16),
        vmem((doms * code_rows, LANES), jnp.int16),
        vmem((doms, LANES), F32),
        vmem((doms, LANES), F32),
        vmem((8 * HALF, LANES), F32),
        vmem((8, LANES), F32),
        vmem((steps, devices, LANES), F32),
        dma((2,)), dma((2,)), dma((doms,)), dma((doms,)),
        dma((steps,)), dma((steps,)),
        dma((doms,)), dma((doms,)), dma((doms,)), dma((doms,)),
    ]
    out = pl.pallas_call(
        functools.partial(kernel, slabs, doms, cap, group),
        out_shape=jax.ShapeDtypeStruct((new_count, V * Q), F32),
        in_specs=[pl.BlockSpec(memory_space=smem)] * 3 + [pl.BlockSpec(memory_space=vmem)]
        + [pl.BlockSpec(memory_space=pltpu.HBM)] * 3,
        out_specs=pl.BlockSpec(memory_space=vmem),
        scratch_shapes=scratch,
        compiler_params=pltpu.CompilerParams(
            collective_id=0, has_side_effects=True, vmem_limit_bytes=56 * 1024 * 1024
        ),
        cost_estimate=pl.CostEstimate(flops=10**9, bytes_accessed=4 * 10**6, transcendentals=0),
    )(
        send_index[0, 0].T, send_count[0], new_order[0], slot_target[0],
        state[0], cross_mass[0, 0], mass[0],
    )
    return out[None]


def solution(mesh):
    in_specs = (
        P("dom", "slab", None),
        P("dom", "slab", None, None),
        P("dom", "slab", None),
        P("dom", "slab", None),
        P("dom", "slab", None, None),
        P("dom", "slab", None),
        P("dom", "slab", None),
    )
    return jax.shard_map(
        functools.partial(per_device, mesh.shape["slab"], mesh.shape["dom"]),
        mesh=mesh, in_specs=in_specs, out_specs=P("dom", "slab", None), check_vma=False,
    )
```

```python
import functools

import jax
import jax.numpy as jnp
from jax import lax
from jax.experimental import pallas as pl
from jax.experimental.pallas import tpu as pltpu
from jax.sharding import PartitionSpec as P

Q = 64
V = 48
RIM = 8
LANES = 128
HALF = V // 2
SUMS = 2
FLOOR = 1e-4
F32 = jnp.float32
BF16 = jnp.bfloat16
LIMIT = 32767.0


def at(index, unit):
    return pl.multiple_of(index * unit, unit)


def left_half(shape):
    return lax.broadcasted_iota(jnp.int32, shape, 1) < Q


def swap(value):
    return pltpu.roll(value, Q, 1)


def interleave(first, second):
    left = left_half(first.shape)
    return jnp.where(left, first, swap(second)), jnp.where(left, swap(first), second)


def split(value):
    high = value.astype(BF16)
    return high, (value - high.astype(F32)).astype(BF16)


def eye(rows):
    shape = (rows, LANES)
    return lax.broadcasted_iota(jnp.int32, shape, 0) == lax.broadcasted_iota(jnp.int32, shape, 1)


def column_to_row(column):
    spread = jnp.where(eye(column.shape[0]), column, 0.0)
    return jnp.sum(spread, axis=0, keepdims=True)


def row_to_column(row, rows):
    spread = jnp.where(eye(rows), row, 0.0)
    return jnp.sum(spread, axis=1, keepdims=True)


def pair_blocks(source, group, block):
    left = left_half((8, LANES))

    def body(t, carry):
        both = source[pl.ds(at(group, 16), 16), pl.ds(at(t, LANES), LANES)].astype(F32)
        first, second = both[:8], both[8:]
        block[pl.ds(2 * t, 8, stride=LANES), :] = jnp.where(left, first, 0.0)
        block[pl.ds(2 * t + 1, 8, stride=LANES), :] = jnp.where(left, swap(first), 0.0)
        block[pl.ds(Q + 2 * t, 8, stride=LANES), :] = jnp.where(left, 0.0, swap(second))
        block[pl.ds(Q + 2 * t + 1, 8, stride=LANES), :] = jnp.where(left, 0.0, second)
        return carry

    lax.fori_loop(0, Q // 2, body, 0, unroll=8)


def kernel(
    slabs, doms, cap, group,
    index_ref, count_ref, order_ref, target_ref, state_hbm, cross_hbm, mass_hbm,
    out_ref,
    state_ref, cross_ref, mass_ref, load_sem,
    pool, up_out, down_out, up_in, down_in, packets, received, block, cross, blocks,
    contrib, residual, image, image2, image3, flat_x, flat_p, flat_r, codes, codes_in, scales, scales_in,
    placed, sums, sums_in,
    halo_send, halo_recv, packet_send, packet_recv, sum_send, sum_recv,
    code_send, code_recv, scale_send, scale_recv,
):
    my_slab, my_dom = lax.axis_index("slab"), lax.axis_index("dom")
    devices = slabs * doms
    me = my_slab * doms + my_dom
    elements = state_ref.shape[0]
    slots = cross_ref.shape[0]
    new_count = mass_ref.shape[0]
    chunk = cap * HALF
    code_rows = codes.shape[0] // doms

    def device(i):
        there = lax.rem(me + i, devices)
        return {"slab": lax.div(there, doms), "dom": lax.rem(there, doms)}

    loads = [
        pltpu.make_async_copy(src, dst, load_sem.at[n])
        for n, (src, dst) in enumerate(
            ((state_hbm, state_ref), (mass_hbm, mass_ref), (cross_hbm, cross_ref))
        )
    ]
    for load in loads:
        load.start()
    barrier = pltpu.get_barrier_semaphore()

    def greet(i, carry):
        pl.semaphore_signal(barrier, inc=1, device_id=device(i), device_id_type=pl.DeviceIdType.MESH)
        return carry

    lax.fori_loop(1, devices, greet, 0)

    loads[0].wait()

    def unfold(t, carry):
        for row in range(0, elements, 16):
            part = state_ref[row:row + 16, pl.ds(at(t, LANES), LANES)].astype(F32)
            pool[pl.ds((RIM + row) * HALF + t, 8, stride=HALF), :] = part[:8]
            pool[pl.ds((RIM + row + 8) * HALF + t, 8, stride=HALF), :] = part[8:]
        return carry

    lax.fori_loop(0, HALF, unfold, 0, unroll=4)
    rim_rows = RIM * HALF
    last = (RIM + elements) * HALF
    down_out[...] = pool[rim_rows:2 * rim_rows, :].astype(BF16)
    up_out[...] = pool[last - rim_rows:last, :].astype(BF16)
    pl.semaphore_wait(barrier, devices - 1)

    def halo(which, src, dst, slab):
        return pltpu.make_async_remote_copy(
            src_ref=src, dst_ref=dst, send_sem=halo_send.at[which], recv_sem=halo_recv.at[which],
            device_id={"slab": slab, "dom": my_dom}, device_id_type=pl.DeviceIdType.MESH,
        )

    up = halo(0, up_out, up_in, lax.rem(my_slab + 1, slabs))
    down = halo(1, down_out, down_in, lax.rem(my_slab + slabs - 1, slabs))

    @pl.when(my_slab < slabs - 1)
    def _():
        up.start()

    @pl.when(my_slab > 0)
    def _():
        down.start()

    loads[1].wait()

    def prepare_mass(j, carry):
        pair_blocks(mass_ref, j, block)

        def cut(i, inner):
            high, low = split(block[pl.ds(at(i, LANES), LANES), :])
            blocks[pl.ds(at(j * 8 + i, LANES), LANES), 0:LANES] = high
            blocks[pl.ds(at(j * 8 + i, LANES), LANES), LANES:2 * LANES] = low
            return inner

        return lax.fori_loop(0, 8, cut, carry, unroll=4)

    lax.fori_loop(0, new_count // 32, prepare_mass, 0)

    @pl.when(my_slab > 0)
    def _():
        up.wait_recv()
        pool[0:rim_rows, :] = up_in[...].astype(F32)

    @pl.when(my_slab == 0)
    def _():
        pool[0:rim_rows, :] = jnp.zeros((rim_rows, LANES), F32)

    @pl.when(my_slab < slabs - 1)
    def _():
        down.wait_recv()
        pool[last:last + rim_rows, :] = down_in[...].astype(F32)

    @pl.when(my_slab == slabs - 1)
    def _():
        pool[last:last + rim_rows, :] = jnp.zeros((rim_rows, LANES), F32)

    def pick(dom):
        live = count_ref[0, dom]
        rows = []
        for c in range(cap):
            row = pool[pl.ds(index_ref[c, dom] * HALF, HALF), :]
            rows.append(row * jnp.minimum(jnp.maximum(live - c, 0), 1).astype(F32))
        return jnp.concatenate(rows, axis=0).astype(BF16)

    def packet(dom):
        return pltpu.make_async_remote_copy(
            src_ref=packets.at[pl.ds(at(dom, chunk), chunk), :],
            dst_ref=received.at[pl.ds(at(my_dom, chunk), chunk), :],
            send_sem=packet_send.at[dom], recv_sem=packet_recv.at[my_dom],
            device_id={"slab": my_slab, "dom": dom}, device_id_type=pl.DeviceIdType.MESH,
        )

    def partner(i):
        return lax.rem(my_dom + 1 + lax.rem(i + doms // 2 - 2, doms - 1), doms)

    def send_packet(i, carry):
        dom = partner(i)
        packets[pl.ds(at(dom, chunk), chunk), :] = pick(dom)
        packet(dom).start()
        return carry

    lax.fori_loop(1, doms, send_packet, 0)
    received[pl.ds(at(my_dom, chunk), chunk), :] = pick(my_dom)

    lax.fori_loop(new_count // 32, new_count // 16, prepare_mass, 0)

    def prepare_cross(j, carry):
        pair_blocks(cross_ref, j, block)

        def cut(i, inner):
            cross[pl.ds(at(j * 8 + i, LANES), LANES), :] = jnp.transpose(
                block[pl.ds(at(i, LANES), LANES), :]
            ).astype(BF16)
            return inner

        return lax.fori_loop(0, 8, cut, carry, unroll=4)

    loads[2].wait()
    lax.fori_loop(0, slots // 16, prepare_cross, 0)

    def arrive(dom, carry):
        @pl.when(dom != my_dom)
        def _():
            pltpu.make_async_remote_copy(
                src_ref=packets.at[pl.ds(at(dom, chunk), chunk), :],
                dst_ref=received.at[pl.ds(at(dom, chunk), chunk), :],
                send_sem=packet_send.at[dom], recv_sem=packet_recv.at[dom],
                device_id={"slab": my_slab, "dom": dom}, device_id_type=pl.DeviceIdType.MESH,
            ).wait()

        return carry

    lax.fori_loop(0, doms, arrive, 0)

    senders = 16 // cap

    def product(step, carry):
        j, h = lax.div(step, senders // 2), lax.rem(step, senders // 2)
        first = received[pl.ds(at(j * senders + h, chunk), chunk), :].astype(F32)
        second = received[pl.ds(at(j * senders + senders // 2 + h, chunk), chunk), :].astype(F32)
        for c in range(cap):
            part = slice(c * HALF, (c + 1) * HALF)
            pair = j * 8 + h * cap + c
            field = jnp.concatenate(interleave(first[part], second[part]), axis=0).astype(BF16)
            matrix = cross[pl.ds(at(pair, LANES), LANES), :]
            contrib[pl.ds(at(pair, V), V), :] = jnp.dot(
                field, matrix, preferred_element_type=F32
            )
        return carry

    lax.fori_loop(0, doms // 2, product, 0, unroll=4)

    shape = (new_count, slots)
    onehot = jnp.where(lax.broadcasted_iota(jnp.int32, shape, 0) == target_ref[...], 1.0, 0.0).astype(BF16)
    pairs_in = slots // 2

    def scatter(t, carry):
        even = contrib[pl.ds(t, pairs_in, stride=V), :]
        odd = contrib[pl.ds(HALF + t, pairs_in, stride=V), :]
        first, second = interleave(even, odd)
        rows = []
        for j in range(pairs_in // 8):
            rows += [first[j * 8:j * 8 + 8], second[j * 8:j * 8 + 8]]
        terms = jnp.concatenate(split(jnp.concatenate(rows, axis=0)), axis=1)
        total = jnp.dot(onehot, terms, preferred_element_type=F32)
        total = total[:, :LANES] + total[:, LANES:]
        for j in range(new_count // 16):
            even, odd = interleave(total[j * 16:j * 16 + 8], total[j * 16 + 8:j * 16 + 16])
            residual[pl.ds(j * 8 * V + t, 8, stride=V), :] = even
            residual[pl.ds(j * 8 * V + HALF + t, 8, stride=V), :] = odd
        return carry

    lax.fori_loop(0, HALF, scatter, 0, unroll=6)

    pairs = new_count // 2

    def apply_mass(pair, field):
        terms = jnp.concatenate(split(field), axis=0)
        result = jnp.dot(terms, blocks[pl.ds(at(pair, LANES), LANES), :], preferred_element_type=F32)
        return (result[V:, :LANES] + result[:V, LANES:]) + result[:V, :LANES]

    def sum_start(step, parts):
        stack = jnp.sum(jnp.concatenate(parts, axis=0), axis=1, keepdims=True)
        half = stack.shape[0] // 2
        own = jnp.concatenate([column_to_row(stack[:half]), column_to_row(stack[half:])], axis=0)
        sums[step] = own

        def send(i, carry):
            pltpu.make_async_remote_copy(
                src_ref=sums.at[step], dst_ref=sums_in.at[step, i - 1],
                send_sem=sum_send.at[step], recv_sem=sum_recv.at[step],
                device_id=device(i), device_id_type=pl.DeviceIdType.MESH,
            ).start()
            return carry

        lax.fori_loop(1, devices, send, 0)
        return own

    def sum_end(step, own, count):
        arrived = sums_in.at[step, 0:devices - 1]
        pltpu.make_async_copy(arrived, arrived, sum_recv.at[step]).wait()
        total = own + jnp.sum(sums_in[step, 0:devices - 1], axis=0)
        half = count * V // 2
        column = jnp.concatenate([row_to_column(total[:1], half), row_to_column(total[1:], half)], axis=0)
        return [column[n * V:(n + 1) * V] for n in range(count)]

    zero = jnp.zeros((V, LANES), F32)
    small = jnp.zeros((HALF, LANES), F32)

    def first_pass(pair, carry):
        bb, bw, ww, wq = carry
        at_pair = pl.ds(at(pair, V), V)
        b = residual[at_pair, :]
        w = apply_mass(pair, b)
        image[at_pair, :] = w
        q = apply_mass(pair, w)
        image2[at_pair, :] = q
        return bb + b * b, bw + b * w, ww + w * w, wq + w * q

    own = sum_start(0, lax.fori_loop(0, pairs, first_pass, (zero,) * 4, unroll=8))

    def third_image(pair, carry):
        at_pair = pl.ds(at(pair, V), V)
        image3[at_pair, :] = apply_mass(pair, image2[at_pair, :])
        return carry

    lax.fori_loop(0, pairs, third_image, 0, unroll=8)
    bb, bw, ww, wq = sum_end(0, own, 4)

    alpha = bb / bw
    norm = alpha * (alpha * ww) - bb
    weighted = bw - 2.0 * (alpha * ww) + alpha * (alpha * wq)
    beta = norm / bb
    curve = weighted - beta * (norm / alpha)
    sound = jnp.logical_and(norm > FLOOR * bb, curve > 0.0)
    beta = jnp.where(sound, beta, 0.0)
    alpha1 = jnp.where(sound, norm / jnp.where(sound, curve, 1.0), alpha)

    dots = []
    for part in range(2):
        rows = slice(part * HALF, (part + 1) * HALF)
        a0, a1, grow = (
            jnp.broadcast_to(value[rows], (HALF, LANES)) for value in (alpha, alpha1, 1.0 + beta)
        )

        def second_pass(pair, carry, part=part, a0=a0, a1=a1, grow=grow):
            rr, rw, rs, ps, rp = carry
            at_pair = pl.ds(at(pair * 2 + part, HALF), HALF)
            b, w, q, t = (ref[at_pair, :] for ref in (residual, image, image2, image3))
            p = grow * b - a0 * w
            s = grow * w - a0 * q
            r = (b - a0 * w) - a1 * s
            v = (w - a0 * q) - a1 * (grow * q - a0 * t)
            image3[at_pair, :] = a0 * b + a1 * p
            image2[at_pair, :] = p
            residual[at_pair, :] = r
            return rr + r * r, rw + r * v, rs + r * s, ps + p * s, rp + r * p

        dots.append(lax.fori_loop(0, pairs, second_pass, (small,) * 5, unroll=4))

    own = sum_start(1, [half for pair in zip(*dots) for half in pair])

    def flatten(pair, carry):
        at_pair = pl.ds(at(pair, V), V)
        number = lax.div(pair, 8) * 16 + lax.rem(pair, 8)
        for src, dst in ((image3, flat_x), (image2, flat_p), (residual, flat_r)):
            value = src[at_pair, :]
            first, second = interleave(value[:HALF], value[HALF:])
            dst[pl.ds(at(number, HALF), HALF), :] = first
            dst[pl.ds(at(number + 8, HALF), HALF), :] = second
        return carry

    lax.fori_loop(0, pairs, flatten, 0, unroll=4)
    rr, rw, rs, ps, rp = sum_end(1, own, 5)
    beta = -rs / ps
    alpha = (rr + beta * rp) / (rw + beta * (2.0 * rs + beta * ps))

    def flat_factor(column):
        wide = jnp.broadcast_to(column, (V, LANES))
        return jnp.where(left_half((HALF, LANES)), wide[:HALF], wide[HALF:])

    factor_r = flat_factor(alpha)
    factor_p = flat_factor(alpha * beta)

    used = group * HALF

    def code(dom):
        rows = []
        for g in range(group):
            which = pl.ds(order_ref[0, dom * group + g] * HALF, HALF)
            rows.append(flat_x[which, :] + (factor_p * flat_p[which, :] + factor_r * flat_r[which, :]))
        value = jnp.concatenate(rows, axis=0)
        top = jnp.maximum(jnp.max(jnp.abs(value), axis=1, keepdims=True), 1e-30)
        coded = jnp.round(value * (LIMIT / top)).astype(jnp.int32)
        if code_rows > used:
            coded = jnp.concatenate([coded, jnp.zeros((code_rows - used, LANES), jnp.int32)], axis=0)
        return coded.astype(jnp.int16), column_to_row(top * (1.0 / LIMIT))

    def code_copies(to, frm, dst):
        where = {"slab": my_slab, "dom": to}
        return [
            pltpu.make_async_remote_copy(
                src_ref=codes.at[pl.ds(at(to, code_rows), code_rows), :],
                dst_ref=codes_in.at[pl.ds(at(dst, code_rows), code_rows), :],
                send_sem=code_send.at[to], recv_sem=code_recv.at[frm],
                device_id=where, device_id_type=pl.DeviceIdType.MESH,
            ),
            pltpu.make_async_remote_copy(
                src_ref=scales.at[pl.ds(to, 1), :], dst_ref=scales_in.at[pl.ds(dst, 1), :],
                send_sem=scale_send.at[to], recv_sem=scale_recv.at[frm],
                device_id=where, device_id_type=pl.DeviceIdType.MESH,
            ),
        ]

    def send_code(i, carry):
        dom = partner(i)
        coded, scale = code(dom)
        codes[pl.ds(at(dom, code_rows), code_rows), :] = coded
        scales[pl.ds(dom, 1), :] = scale
        for copy in code_copies(dom, my_dom, my_dom):
            copy.start()
        return carry

    lax.fori_loop(1, doms, send_code, 0)
    coded, scale = code(my_dom)
    codes_in[pl.ds(at(my_dom, code_rows), code_rows), :] = coded
    scales_in[pl.ds(my_dom, 1), :] = scale

    def place(rows, carry):
        for n in range(8 // group):
            dom = rows * (8 // group) + n

            @pl.when(dom != my_dom)
            def _():
                for copy in code_copies(dom, dom, dom):
                    copy.wait()

            value = codes_in[pl.ds(at(dom, code_rows), code_rows), :].astype(jnp.int32).astype(F32)[:used]
            scale = row_to_column(scales_in[pl.ds(dom, 1), :], used)
            placed[n * used:(n + 1) * used, :] = value * scale
        for t in range(HALF):
            out_ref[pl.ds(at(rows, 8), 8), t * LANES:(t + 1) * LANES] = placed[pl.ds(t, 8, stride=HALF), :]
        return carry

    lax.fori_loop(0, new_count // 8, place, 0)

    for step in range(SUMS):
        left = sums_in.at[step, 0:devices - 1]
        pltpu.make_async_copy(left, left, sum_send.at[step]).wait()

    @pl.when(my_slab < slabs - 1)
    def _():
        up.wait_send()

    @pl.when(my_slab > 0)
    def _():
        down.wait_send()


def move_kernel(src, dst, sem):
    rows = src.shape[0] // 8
    copies = [
        pltpu.make_async_copy(
            src.at[n * rows:(n + 1) * rows, :], dst.at[n * rows:(n + 1) * rows, :], sem.at[n]
        )
        for n in range(8)
    ]
    for copy in copies:
        copy.start()
    for copy in copies:
        copy.wait()


def move(value):
    return pl.pallas_call(
        move_kernel,
        out_shape=jax.ShapeDtypeStruct(value.shape, value.dtype),
        in_specs=[pl.BlockSpec(memory_space=pl.ANY)],
        out_specs=pl.BlockSpec(memory_space=pl.ANY),
        scratch_shapes=[pltpu.SemaphoreType.DMA((8,))],
        compiler_params=pltpu.CompilerParams(vmem_limit_bytes=56 * 1024 * 1024),
    )(value)


def per_device(slabs, doms, state, send_index, send_count, slot_target, cross_mass, mass, new_order):
    cap = send_index.shape[3]
    new_count = mass.shape[1]
    group = new_count // doms
    slots = doms * cap
    pool_rows = (state.shape[1] + 2 * RIM) * HALF
    rim_rows = RIM * HALF
    code_rows = -(-group * HALF // 16) * 16
    devices = slabs * doms
    steps = SUMS
    vmem, smem = pltpu.VMEM, pltpu.SMEM
    dma = pltpu.SemaphoreType.DMA
    field = vmem((new_count * HALF, LANES), F32)
    scratch = [
        vmem(state.shape[1:], BF16),
        vmem((slots, Q * Q), BF16),
        vmem((new_count, Q * Q), F32),
        dma((3,)),
        vmem((pool_rows, LANES), F32),
        *[vmem((rim_rows, LANES), BF16)] * 4,
        vmem((slots * HALF, LANES), BF16),
        vmem((slots * HALF, LANES), BF16),
        vmem((8 * LANES, LANES), F32),
        vmem((slots // 2 * LANES, LANES), BF16),
        vmem((new_count // 2 * LANES, 2 * LANES), BF16),
        vmem((slots * HALF, LANES), F32),
        *[field] * 7,
        vmem((doms * code_rows, LANES), jnp.int16),
        vmem((doms * code_rows, LANES), jnp.int16),
        vmem((doms, LANES), F32),
        vmem((doms, LANES), F32),
        vmem((8 * HALF, LANES), F32),
        vmem((steps, 2, LANES), F32),
        vmem((steps, devices, 2, LANES), F32),
        dma((2,)), dma((2,)), dma((doms,)), dma((doms,)),
        dma((steps,)), dma((steps,)),
        dma((doms,)), dma((doms,)), dma((doms,)), dma((doms,)),
    ]
    out = pl.pallas_call(
        functools.partial(kernel, slabs, doms, cap, group),
        out_shape=jax.ShapeDtypeStruct((new_count, V * Q), F32),
        in_specs=[pl.BlockSpec(memory_space=smem)] * 3 + [pl.BlockSpec(memory_space=vmem)]
        + [pl.BlockSpec(memory_space=pltpu.HBM)] * 3,
        out_specs=pl.BlockSpec(memory_space=vmem),
        scratch_shapes=scratch,
        compiler_params=pltpu.CompilerParams(
            collective_id=0, has_side_effects=True, vmem_limit_bytes=56 * 1024 * 1024
        ),
        cost_estimate=pl.CostEstimate(flops=10**9, bytes_accessed=4 * 10**6, transcendentals=0),
    )(
        send_index[0, 0].T, send_count[0], new_order[0], slot_target[0],
        state[0], cross_mass[0, 0], mass[0],
    )
    return move(out)[None]


def solution(mesh):
    in_specs = (
        P("dom", "slab", None),
        P("dom", "slab", None, None),
        P("dom", "slab", None),
        P("dom", "slab", None),
        P("dom", "slab", None, None),
        P("dom", "slab", None),
        P("dom", "slab", None),
    )
    return jax.shard_map(
        functools.partial(per_device, mesh.shape["slab"], mesh.shape["dom"]),
        mesh=mesh, in_specs=in_specs, out_specs=P("dom", "slab", None), check_vma=False,
    )
```

```python
import functools

import jax
import jax.numpy as jnp
from jax import lax
from jax.experimental import pallas as pl
from jax.experimental.pallas import tpu as pltpu
from jax.sharding import PartitionSpec as P

Q = 64
V = 48
RIM = 8
LANES = 128
HALF = V // 2
SUMS = 2
FLOOR = 1e-4
F32 = jnp.float32
BF16 = jnp.bfloat16
LIMIT = 32767.0


def at(index, unit):
    return pl.multiple_of(index * unit, unit)


def left_half(shape):
    return lax.broadcasted_iota(jnp.int32, shape, 1) < Q


def swap(value):
    return pltpu.roll(value, Q, 1)


def interleave(first, second):
    left = left_half(first.shape)
    return jnp.where(left, first, swap(second)), jnp.where(left, swap(first), second)


def split(value):
    high = value.astype(BF16)
    return high, (value - high.astype(F32)).astype(BF16)


def eye(rows):
    shape = (rows, LANES)
    return lax.broadcasted_iota(jnp.int32, shape, 0) == lax.broadcasted_iota(jnp.int32, shape, 1)


def column_to_row(column):
    spread = jnp.where(eye(column.shape[0]), column, 0.0)
    return jnp.sum(spread, axis=0, keepdims=True)


def row_to_column(row, rows):
    spread = jnp.where(eye(rows), row, 0.0)
    return jnp.sum(spread, axis=1, keepdims=True)


def pair_blocks(source, group, block):
    left = left_half((8, LANES))

    def body(t, carry):
        both = source[pl.ds(at(group, 16), 16), pl.ds(at(t, LANES), LANES)].astype(F32)
        first, second = both[:8], both[8:]
        block[pl.ds(2 * t, 8, stride=LANES), :] = jnp.where(left, first, 0.0)
        block[pl.ds(2 * t + 1, 8, stride=LANES), :] = jnp.where(left, swap(first), 0.0)
        block[pl.ds(Q + 2 * t, 8, stride=LANES), :] = jnp.where(left, 0.0, swap(second))
        block[pl.ds(Q + 2 * t + 1, 8, stride=LANES), :] = jnp.where(left, 0.0, second)
        return carry

    lax.fori_loop(0, Q // 2, body, 0, unroll=8)


def kernel(
    slabs, doms, cap, group,
    index_ref, count_ref, order_ref, target_ref, state_hbm, cross_hbm, mass_hbm,
    out_ref,
    state_ref, cross_ref, mass_ref, load_sem,
    pool, up_out, down_out, up_in, down_in, packets, received, block, cross, blocks,
    contrib, residual, image, image2, image3, flat_x, flat_p, flat_r, codes, codes_in, scales, scales_in,
    placed, sums, sums_in,
    halo_send, halo_recv, packet_send, packet_recv, sum_send, sum_recv,
    code_send, code_recv, scale_send, scale_recv,
):
    my_slab, my_dom = lax.axis_index("slab"), lax.axis_index("dom")
    devices = slabs * doms
    me = my_slab * doms + my_dom
    elements = state_ref.shape[0]
    slots = cross_ref.shape[0]
    new_count = mass_ref.shape[0]
    chunk = cap * HALF
    code_rows = codes.shape[0] // doms

    def device(i):
        there = lax.rem(me + i, devices)
        return {"slab": lax.div(there, doms), "dom": lax.rem(there, doms)}

    loads = [
        pltpu.make_async_copy(src, dst, load_sem.at[n])
        for n, (src, dst) in enumerate(
            ((state_hbm, state_ref), (mass_hbm, mass_ref), (cross_hbm, cross_ref))
        )
    ]
    for load in loads:
        load.start()
    barrier = pltpu.get_barrier_semaphore()

    def greet(i, carry):
        pl.semaphore_signal(barrier, inc=1, device_id=device(i), device_id_type=pl.DeviceIdType.MESH)
        return carry

    lax.fori_loop(1, devices, greet, 0)

    loads[0].wait()

    def unfold(t, carry):
        for row in range(0, elements, 16):
            part = state_ref[row:row + 16, pl.ds(at(t, LANES), LANES)].astype(F32)
            pool[pl.ds((RIM + row) * HALF + t, 8, stride=HALF), :] = part[:8]
            pool[pl.ds((RIM + row + 8) * HALF + t, 8, stride=HALF), :] = part[8:]
        return carry

    lax.fori_loop(0, HALF, unfold, 0, unroll=4)
    rim_rows = RIM * HALF
    last = (RIM + elements) * HALF
    down_out[...] = pool[rim_rows:2 * rim_rows, :].astype(BF16)
    up_out[...] = pool[last - rim_rows:last, :].astype(BF16)
    pl.semaphore_wait(barrier, devices - 1)

    def halo(which, src, dst, slab):
        return pltpu.make_async_remote_copy(
            src_ref=src, dst_ref=dst, send_sem=halo_send.at[which], recv_sem=halo_recv.at[which],
            device_id={"slab": slab, "dom": my_dom}, device_id_type=pl.DeviceIdType.MESH,
        )

    up = halo(0, up_out, up_in, lax.rem(my_slab + 1, slabs))
    down = halo(1, down_out, down_in, lax.rem(my_slab + slabs - 1, slabs))

    @pl.when(my_slab < slabs - 1)
    def _():
        up.start()

    @pl.when(my_slab > 0)
    def _():
        down.start()

    loads[1].wait()

    def prepare_mass(j, carry):
        pair_blocks(mass_ref, j, block)

        def cut(i, inner):
            high, low = split(block[pl.ds(at(i, LANES), LANES), :])
            blocks[pl.ds(at(j * 8 + i, LANES), LANES), 0:LANES] = high
            blocks[pl.ds(at(j * 8 + i, LANES), LANES), LANES:2 * LANES] = low
            return inner

        return lax.fori_loop(0, 8, cut, carry, unroll=4)

    lax.fori_loop(0, new_count // 32, prepare_mass, 0)

    @pl.when(my_slab > 0)
    def _():
        up.wait_recv()
        pool[0:rim_rows, :] = up_in[...].astype(F32)

    @pl.when(my_slab == 0)
    def _():
        pool[0:rim_rows, :] = jnp.zeros((rim_rows, LANES), F32)

    @pl.when(my_slab < slabs - 1)
    def _():
        down.wait_recv()
        pool[last:last + rim_rows, :] = down_in[...].astype(F32)

    @pl.when(my_slab == slabs - 1)
    def _():
        pool[last:last + rim_rows, :] = jnp.zeros((rim_rows, LANES), F32)

    def pick(dom):
        live = count_ref[0, dom]
        rows = []
        for c in range(cap):
            row = pool[pl.ds(index_ref[c, dom] * HALF, HALF), :]
            rows.append(row * jnp.minimum(jnp.maximum(live - c, 0), 1).astype(F32))
        return jnp.concatenate(rows, axis=0).astype(BF16)

    def packet(dom):
        return pltpu.make_async_remote_copy(
            src_ref=packets.at[pl.ds(at(dom, chunk), chunk), :],
            dst_ref=received.at[pl.ds(at(my_dom, chunk), chunk), :],
            send_sem=packet_send.at[dom], recv_sem=packet_recv.at[my_dom],
            device_id={"slab": my_slab, "dom": dom}, device_id_type=pl.DeviceIdType.MESH,
        )

    def partner(i):
        apart = lax.rem(i, 2) * (doms // 2) + lax.div(i, 2)
        if doms & (doms - 1):
            return lax.rem(my_dom + apart, doms)
        other, bit = 0, 1
        while bit < doms:
            differ = lax.rem(lax.div(my_dom, bit) + lax.div(apart, bit), 2)
            other, bit = other + differ * bit, bit * 2
        return other

    def send_packet(i, carry):
        dom = partner(i)
        packets[pl.ds(at(dom, chunk), chunk), :] = pick(dom)
        packet(dom).start()
        return carry

    lax.fori_loop(1, doms, send_packet, 0)
    received[pl.ds(at(my_dom, chunk), chunk), :] = pick(my_dom)

    lax.fori_loop(new_count // 32, new_count // 16, prepare_mass, 0)

    def prepare_cross(j, carry):
        pair_blocks(cross_ref, j, block)

        def cut(i, inner):
            cross[pl.ds(at(j * 8 + i, LANES), LANES), :] = jnp.transpose(
                block[pl.ds(at(i, LANES), LANES), :]
            ).astype(BF16)
            return inner

        return lax.fori_loop(0, 8, cut, carry, unroll=4)

    loads[2].wait()
    lax.fori_loop(0, slots // 16, prepare_cross, 0)

    def arrive(dom, carry):
        @pl.when(dom != my_dom)
        def _():
            pltpu.make_async_remote_copy(
                src_ref=packets.at[pl.ds(at(dom, chunk), chunk), :],
                dst_ref=received.at[pl.ds(at(dom, chunk), chunk), :],
                send_sem=packet_send.at[dom], recv_sem=packet_recv.at[dom],
                device_id={"slab": my_slab, "dom": dom}, device_id_type=pl.DeviceIdType.MESH,
            ).wait()

        return carry

    lax.fori_loop(0, doms, arrive, 0)

    senders = 16 // cap

    def product(step, carry):
        j, h = lax.div(step, senders // 2), lax.rem(step, senders // 2)
        first = received[pl.ds(at(j * senders + h, chunk), chunk), :].astype(F32)
        second = received[pl.ds(at(j * senders + senders // 2 + h, chunk), chunk), :].astype(F32)
        for c in range(cap):
            part = slice(c * HALF, (c + 1) * HALF)
            pair = j * 8 + h * cap + c
            field = jnp.concatenate(interleave(first[part], second[part]), axis=0).astype(BF16)
            matrix = cross[pl.ds(at(pair, LANES), LANES), :]
            contrib[pl.ds(at(pair, V), V), :] = jnp.dot(
                field, matrix, preferred_element_type=F32
            )
        return carry

    lax.fori_loop(0, doms // 2, product, 0, unroll=4)

    shape = (new_count, slots)
    onehot = jnp.where(lax.broadcasted_iota(jnp.int32, shape, 0) == target_ref[...], 1.0, 0.0).astype(BF16)
    pairs_in = slots // 2

    def scatter(t, carry):
        even = contrib[pl.ds(t, pairs_in, stride=V), :]
        odd = contrib[pl.ds(HALF + t, pairs_in, stride=V), :]
        first, second = interleave(even, odd)
        rows = []
        for j in range(pairs_in // 8):
            rows += [first[j * 8:j * 8 + 8], second[j * 8:j * 8 + 8]]
        terms = jnp.concatenate(split(jnp.concatenate(rows, axis=0)), axis=1)
        total = jnp.dot(onehot, terms, preferred_element_type=F32)
        total = total[:, :LANES] + total[:, LANES:]
        for j in range(new_count // 16):
            even, odd = interleave(total[j * 16:j * 16 + 8], total[j * 16 + 8:j * 16 + 16])
            residual[pl.ds(j * 8 * V + t, 8, stride=V), :] = even
            residual[pl.ds(j * 8 * V + HALF + t, 8, stride=V), :] = odd
        return carry

    lax.fori_loop(0, HALF, scatter, 0, unroll=6)

    pairs = new_count // 2

    def apply_mass(pair, field):
        terms = jnp.concatenate(split(field), axis=0)
        result = jnp.dot(terms, blocks[pl.ds(at(pair, LANES), LANES), :], preferred_element_type=F32)
        return (result[V:, :LANES] + result[:V, LANES:]) + result[:V, :LANES]

    def sum_start(step, parts):
        stack = jnp.sum(jnp.concatenate(parts, axis=0), axis=1, keepdims=True)
        half = stack.shape[0] // 2
        own = jnp.concatenate([column_to_row(stack[:half]), column_to_row(stack[half:])], axis=0)
        sums[step] = own

        def send(i, carry):
            pltpu.make_async_remote_copy(
                src_ref=sums.at[step], dst_ref=sums_in.at[step, i - 1],
                send_sem=sum_send.at[step], recv_sem=sum_recv.at[step],
                device_id=device(i), device_id_type=pl.DeviceIdType.MESH,
            ).start()
            return carry

        lax.fori_loop(1, devices, send, 0)
        return own

    def sum_end(step, own, count):
        arrived = sums_in.at[step, 0:devices - 1]
        pltpu.make_async_copy(arrived, arrived, sum_recv.at[step]).wait()
        total = own + jnp.sum(sums_in[step, 0:devices - 1], axis=0)
        half = count * V // 2
        column = jnp.concatenate([row_to_column(total[:1], half), row_to_column(total[1:], half)], axis=0)
        return [column[n * V:(n + 1) * V] for n in range(count)]

    zero = jnp.zeros((V, LANES), F32)
    small = jnp.zeros((HALF, LANES), F32)

    def first_pass(pair, carry):
        bb, bw, ww, wq = carry
        at_pair = pl.ds(at(pair, V), V)
        b = residual[at_pair, :]
        w = apply_mass(pair, b)
        image[at_pair, :] = w
        q = apply_mass(pair, w)
        image2[at_pair, :] = q
        return bb + b * b, bw + b * w, ww + w * w, wq + w * q

    own = sum_start(0, lax.fori_loop(0, pairs, first_pass, (zero,) * 4, unroll=8))

    def third_image(pair, carry):
        at_pair = pl.ds(at(pair, V), V)
        image3[at_pair, :] = apply_mass(pair, image2[at_pair, :])
        return carry

    lax.fori_loop(0, pairs, third_image, 0, unroll=8)
    bb, bw, ww, wq = sum_end(0, own, 4)

    alpha = bb / bw
    norm = alpha * (alpha * ww) - bb
    weighted = bw - 2.0 * (alpha * ww) + alpha * (alpha * wq)
    beta = norm / bb
    curve = weighted - beta * (norm / alpha)
    sound = jnp.logical_and(norm > FLOOR * bb, curve > 0.0)
    beta = jnp.where(sound, beta, 0.0)
    alpha1 = jnp.where(sound, norm / jnp.where(sound, curve, 1.0), alpha)

    dots = []
    for part in range(2):
        rows = slice(part * HALF, (part + 1) * HALF)
        a0, a1, grow = (
            jnp.broadcast_to(value[rows], (HALF, LANES)) for value in (alpha, alpha1, 1.0 + beta)
        )

        def second_pass(pair, carry, part=part, a0=a0, a1=a1, grow=grow):
            rr, rw, rs, ps, rp = carry
            at_pair = pl.ds(at(pair * 2 + part, HALF), HALF)
            b, w, q, t = (ref[at_pair, :] for ref in (residual, image, image2, image3))
            p = grow * b - a0 * w
            s = grow * w - a0 * q
            r = (b - a0 * w) - a1 * s
            v = (w - a0 * q) - a1 * (grow * q - a0 * t)
            image3[at_pair, :] = a0 * b + a1 * p
            image2[at_pair, :] = p
            residual[at_pair, :] = r
            return rr + r * r, rw + r * v, rs + r * s, ps + p * s, rp + r * p

        dots.append(lax.fori_loop(0, pairs, second_pass, (small,) * 5, unroll=4))

    own = sum_start(1, [half for pair in zip(*dots) for half in pair])

    def flatten(pair, carry):
        at_pair = pl.ds(at(pair, V), V)
        number = lax.div(pair, 8) * 16 + lax.rem(pair, 8)
        for src, dst in ((image3, flat_x), (image2, flat_p), (residual, flat_r)):
            value = src[at_pair, :]
            first, second = interleave(value[:HALF], value[HALF:])
            dst[pl.ds(at(number, HALF), HALF), :] = first
            dst[pl.ds(at(number + 8, HALF), HALF), :] = second
        return carry

    lax.fori_loop(0, pairs, flatten, 0, unroll=4)
    rr, rw, rs, ps, rp = sum_end(1, own, 5)
    beta = -rs / ps
    alpha = (rr + beta * rp) / (rw + beta * (2.0 * rs + beta * ps))

    def flat_factor(column):
        wide = jnp.broadcast_to(column, (V, LANES))
        return jnp.where(left_half((HALF, LANES)), wide[:HALF], wide[HALF:])

    factor_r = flat_factor(alpha)
    factor_p = flat_factor(alpha * beta)

    used = group * HALF

    def code(dom):
        rows = []
        for g in range(group):
            which = pl.ds(order_ref[0, dom * group + g] * HALF, HALF)
            rows.append(flat_x[which, :] + (factor_p * flat_p[which, :] + factor_r * flat_r[which, :]))
        value = jnp.concatenate(rows, axis=0)
        top = jnp.maximum(jnp.max(jnp.abs(value), axis=1, keepdims=True), 1e-30)
        coded = jnp.round(value * (LIMIT / top)).astype(jnp.int32)
        if code_rows > used:
            coded = jnp.concatenate([coded, jnp.zeros((code_rows - used, LANES), jnp.int32)], axis=0)
        return coded.astype(jnp.int16), column_to_row(top * (1.0 / LIMIT))

    def code_copies(to, frm, dst):
        where = {"slab": my_slab, "dom": to}
        return [
            pltpu.make_async_remote_copy(
                src_ref=codes.at[pl.ds(at(to, code_rows), code_rows), :],
                dst_ref=codes_in.at[pl.ds(at(dst, code_rows), code_rows), :],
                send_sem=code_send.at[to], recv_sem=code_recv.at[frm],
                device_id=where, device_id_type=pl.DeviceIdType.MESH,
            ),
            pltpu.make_async_remote_copy(
                src_ref=scales.at[pl.ds(to, 1), :], dst_ref=scales_in.at[pl.ds(dst, 1), :],
                send_sem=scale_send.at[to], recv_sem=scale_recv.at[frm],
                device_id=where, device_id_type=pl.DeviceIdType.MESH,
            ),
        ]

    def send_code(i, carry):
        dom = partner(i)
        coded, scale = code(dom)
        codes[pl.ds(at(dom, code_rows), code_rows), :] = coded
        scales[pl.ds(dom, 1), :] = scale
        for copy in code_copies(dom, my_dom, my_dom):
            copy.start()
        return carry

    lax.fori_loop(1, doms, send_code, 0)
    coded, scale = code(my_dom)
    codes_in[pl.ds(at(my_dom, code_rows), code_rows), :] = coded
    scales_in[pl.ds(my_dom, 1), :] = scale

    def place(rows, carry):
        for n in range(8 // group):
            dom = rows * (8 // group) + n

            @pl.when(dom != my_dom)
            def _():
                for copy in code_copies(dom, dom, dom):
                    copy.wait()

            value = codes_in[pl.ds(at(dom, code_rows), code_rows), :].astype(jnp.int32).astype(F32)[:used]
            scale = row_to_column(scales_in[pl.ds(dom, 1), :], used)
            placed[n * used:(n + 1) * used, :] = value * scale
        for t in range(HALF):
            out_ref[pl.ds(at(rows, 8), 8), t * LANES:(t + 1) * LANES] = placed[pl.ds(t, 8, stride=HALF), :]
        return carry

    lax.fori_loop(0, new_count // 8, place, 0)

    for step in range(SUMS):
        left = sums_in.at[step, 0:devices - 1]
        pltpu.make_async_copy(left, left, sum_send.at[step]).wait()

    @pl.when(my_slab < slabs - 1)
    def _():
        up.wait_send()

    @pl.when(my_slab > 0)
    def _():
        down.wait_send()


def move_kernel(src, dst, held, load_sem, store_sem):
    rows = src.shape[0] // 8
    parts = [slice(n * rows, (n + 1) * rows) for n in range(8)]
    loads = [
        pltpu.make_async_copy(src.at[part, :], held.at[part, :], load_sem.at[n])
        for n, part in enumerate(parts)
    ]
    stores = [
        pltpu.make_async_copy(held.at[part, :], dst.at[part, :], store_sem.at[n])
        for n, part in enumerate(parts)
    ]
    for load in loads:
        load.start()
    for load, store in zip(loads, stores):
        load.wait()
        store.start()
    for store in stores:
        store.wait()


def move(value):
    return pl.pallas_call(
        move_kernel,
        out_shape=jax.ShapeDtypeStruct(value.shape, value.dtype),
        in_specs=[pl.BlockSpec(memory_space=pl.ANY)],
        out_specs=pl.BlockSpec(memory_space=pl.ANY),
        scratch_shapes=[
            pltpu.VMEM(value.shape, value.dtype),
            pltpu.SemaphoreType.DMA((8,)),
            pltpu.SemaphoreType.DMA((8,)),
        ],
        compiler_params=pltpu.CompilerParams(vmem_limit_bytes=56 * 1024 * 1024),
    )(value)


def per_device(slabs, doms, state, send_index, send_count, slot_target, cross_mass, mass, new_order):
    cap = send_index.shape[3]
    new_count = mass.shape[1]
    group = new_count // doms
    slots = doms * cap
    pool_rows = (state.shape[1] + 2 * RIM) * HALF
    rim_rows = RIM * HALF
    code_rows = -(-group * HALF // 16) * 16
    devices = slabs * doms
    steps = SUMS
    vmem, smem = pltpu.VMEM, pltpu.SMEM
    dma = pltpu.SemaphoreType.DMA
    field = vmem((new_count * HALF, LANES), F32)
    scratch = [
        vmem(state.shape[1:], BF16),
        vmem((slots, Q * Q), BF16),
        vmem((new_count, Q * Q), F32),
        dma((3,)),
        vmem((pool_rows, LANES), F32),
        *[vmem((rim_rows, LANES), BF16)] * 4,
        vmem((slots * HALF, LANES), BF16),
        vmem((slots * HALF, LANES), BF16),
        vmem((8 * LANES, LANES), F32),
        vmem((slots // 2 * LANES, LANES), BF16),
        vmem((new_count // 2 * LANES, 2 * LANES), BF16),
        vmem((slots * HALF, LANES), F32),
        *[field] * 7,
        vmem((doms * code_rows, LANES), jnp.int16),
        vmem((doms * code_rows, LANES), jnp.int16),
        vmem((doms, LANES), F32),
        vmem((doms, LANES), F32),
        vmem((8 * HALF, LANES), F32),
        vmem((steps, 2, LANES), F32),
        vmem((steps, devices, 2, LANES), F32),
        dma((2,)), dma((2,)), dma((doms,)), dma((doms,)),
        dma((steps,)), dma((steps,)),
        dma((doms,)), dma((doms,)), dma((doms,)), dma((doms,)),
    ]
    out = pl.pallas_call(
        functools.partial(kernel, slabs, doms, cap, group),
        out_shape=jax.ShapeDtypeStruct((new_count, V * Q), F32),
        in_specs=[pl.BlockSpec(memory_space=smem)] * 3 + [pl.BlockSpec(memory_space=vmem)]
        + [pl.BlockSpec(memory_space=pltpu.HBM)] * 3,
        out_specs=pl.BlockSpec(memory_space=vmem),
        scratch_shapes=scratch,
        compiler_params=pltpu.CompilerParams(
            collective_id=0, has_side_effects=True, vmem_limit_bytes=56 * 1024 * 1024
        ),
        cost_estimate=pl.CostEstimate(flops=10**9, bytes_accessed=4 * 10**6, transcendentals=0),
    )(
        send_index[0, 0].T, send_count[0], new_order[0], slot_target[0],
        state[0], cross_mass[0, 0], mass[0],
    )
    return move(out)[None]


def solution(mesh):
    in_specs = (
        P("dom", "slab", None),
        P("dom", "slab", None, None),
        P("dom", "slab", None),
        P("dom", "slab", None),
        P("dom", "slab", None, None),
        P("dom", "slab", None),
        P("dom", "slab", None),
    )
    return jax.shard_map(
        functools.partial(per_device, mesh.shape["slab"], mesh.shape["dom"]),
        mesh=mesh, in_specs=in_specs, out_specs=P("dom", "slab", None), check_vma=False,
    )
```

```python
import functools

import jax
import jax.numpy as jnp
from jax import lax
from jax.experimental import pallas as pl
from jax.experimental.pallas import tpu as pltpu
from jax.sharding import PartitionSpec as P

Q = 64
V = 48
RIM = 8
LANES = 128
HALF = V // 2
SUMS = 2
FLOOR = 1e-4
F32 = jnp.float32
BF16 = jnp.bfloat16
LIMIT = 32767.0


def at(index, unit):
    return pl.multiple_of(index * unit, unit)


def left_half(shape):
    return lax.broadcasted_iota(jnp.int32, shape, 1) < Q


def swap(value):
    return pltpu.roll(value, Q, 1)


def interleave(first, second):
    left = left_half(first.shape)
    return jnp.where(left, first, swap(second)), jnp.where(left, swap(first), second)


def split(value):
    high = value.astype(BF16)
    return high, (value - high.astype(F32)).astype(BF16)


def eye(rows):
    shape = (rows, LANES)
    return lax.broadcasted_iota(jnp.int32, shape, 0) == lax.broadcasted_iota(jnp.int32, shape, 1)


def column_to_row(column):
    spread = jnp.where(eye(column.shape[0]), column, 0.0)
    return jnp.sum(spread, axis=0, keepdims=True)


def row_to_column(row, rows):
    spread = jnp.where(eye(rows), row, 0.0)
    return jnp.sum(spread, axis=1, keepdims=True)


def pair_blocks(source, group, block):
    left = left_half((8, LANES))

    def body(t, carry):
        both = source[pl.ds(at(group, 16), 16), pl.ds(at(t, LANES), LANES)].astype(F32)
        first, second = both[:8], both[8:]
        block[pl.ds(2 * t, 8, stride=LANES), :] = jnp.where(left, first, 0.0)
        block[pl.ds(2 * t + 1, 8, stride=LANES), :] = jnp.where(left, swap(first), 0.0)
        block[pl.ds(Q + 2 * t, 8, stride=LANES), :] = jnp.where(left, 0.0, swap(second))
        block[pl.ds(Q + 2 * t + 1, 8, stride=LANES), :] = jnp.where(left, 0.0, second)
        return carry

    lax.fori_loop(0, Q // 2, body, 0, unroll=8)


def kernel(
    slabs, doms, cap, group,
    index_ref, count_ref, order_ref, target_ref, state_hbm, cross_hbm, mass_hbm,
    codes_out, scales_out,
    state_ref, cross_ref, mass_ref, load_sem,
    pool, up_out, down_out, up_in, down_in, packets, received, block, cross, blocks,
    contrib, residual, image, image2, image3, flat_x, flat_p, flat_r, codes, codes_in, scales, scales_in,
    sums, sums_in,
    halo_send, halo_recv, packet_send, packet_recv, sum_send, sum_recv,
    code_send, code_recv, scale_send, scale_recv,
):
    my_slab, my_dom = lax.axis_index("slab"), lax.axis_index("dom")
    devices = slabs * doms
    elements = state_ref.shape[0]
    slots = cross_ref.shape[0]
    new_count = mass_ref.shape[0]
    chunk = cap * HALF
    code_rows = codes.shape[0] // doms

    def wrap(value, size):
        return jnp.where(value >= size, value - size, value)

    def each_device(act):
        for apart in range(slabs):
            slab = wrap(my_slab + apart, slabs)

            def body(i, carry, apart=apart, slab=slab):
                act(apart * doms + i - 1, {"slab": slab, "dom": wrap(my_dom + i, doms)})
                return carry

            lax.fori_loop(1 if apart == 0 else 0, doms, body, 0, unroll=3 if apart == 0 else 4)

    loads = [
        pltpu.make_async_copy(src, dst, load_sem.at[n])
        for n, (src, dst) in enumerate(
            ((state_hbm, state_ref), (mass_hbm, mass_ref), (cross_hbm, cross_ref))
        )
    ]
    for load in loads:
        load.start()
    barrier = pltpu.get_barrier_semaphore()

    def greet(i, where):
        pl.semaphore_signal(barrier, inc=1, device_id=where, device_id_type=pl.DeviceIdType.MESH)

    each_device(greet)

    loads[0].wait()

    def unfold(t, carry):
        for row in range(0, elements, 16):
            part = state_ref[row:row + 16, pl.ds(at(t, LANES), LANES)].astype(F32)
            pool[pl.ds((RIM + row) * HALF + t, 8, stride=HALF), :] = part[:8]
            pool[pl.ds((RIM + row + 8) * HALF + t, 8, stride=HALF), :] = part[8:]
        return carry

    lax.fori_loop(0, HALF, unfold, 0, unroll=4)
    rim_rows = RIM * HALF
    last = (RIM + elements) * HALF
    down_out[...] = pool[rim_rows:2 * rim_rows, :].astype(BF16)
    up_out[...] = pool[last - rim_rows:last, :].astype(BF16)
    pl.semaphore_wait(barrier, devices - 1)

    def halo(which, src, dst, slab):
        return pltpu.make_async_remote_copy(
            src_ref=src, dst_ref=dst, send_sem=halo_send.at[which], recv_sem=halo_recv.at[which],
            device_id={"slab": slab, "dom": my_dom}, device_id_type=pl.DeviceIdType.MESH,
        )

    up = halo(0, up_out, up_in, lax.rem(my_slab + 1, slabs))
    down = halo(1, down_out, down_in, lax.rem(my_slab + slabs - 1, slabs))

    @pl.when(my_slab < slabs - 1)
    def _():
        up.start()

    @pl.when(my_slab > 0)
    def _():
        down.start()

    loads[1].wait()

    def prepare_mass(j, carry):
        pair_blocks(mass_ref, j, block)

        def cut(i, inner):
            high, low = split(block[pl.ds(at(i, LANES), LANES), :])
            blocks[pl.ds(at(j * 8 + i, LANES), LANES), 0:LANES] = high
            blocks[pl.ds(at(j * 8 + i, LANES), LANES), LANES:2 * LANES] = low
            return inner

        return lax.fori_loop(0, 8, cut, carry, unroll=4)

    lax.fori_loop(0, new_count // 32, prepare_mass, 0)

    @pl.when(my_slab > 0)
    def _():
        up.wait_recv()
        pool[0:rim_rows, :] = up_in[...].astype(F32)

    @pl.when(my_slab == 0)
    def _():
        pool[0:rim_rows, :] = jnp.zeros((rim_rows, LANES), F32)

    @pl.when(my_slab < slabs - 1)
    def _():
        down.wait_recv()
        pool[last:last + rim_rows, :] = down_in[...].astype(F32)

    @pl.when(my_slab == slabs - 1)
    def _():
        pool[last:last + rim_rows, :] = jnp.zeros((rim_rows, LANES), F32)

    def pick(dom):
        live = count_ref[0, dom]
        rows = []
        for c in range(cap):
            row = pool[pl.ds(index_ref[c, dom] * HALF, HALF), :]
            rows.append(row * jnp.minimum(jnp.maximum(live - c, 0), 1).astype(F32))
        return jnp.concatenate(rows, axis=0).astype(BF16)

    def packet(dom):
        return pltpu.make_async_remote_copy(
            src_ref=packets.at[pl.ds(at(dom, chunk), chunk), :],
            dst_ref=received.at[pl.ds(at(my_dom, chunk), chunk), :],
            send_sem=packet_send.at[dom], recv_sem=packet_recv.at[my_dom],
            device_id={"slab": my_slab, "dom": dom}, device_id_type=pl.DeviceIdType.MESH,
        )

    def partner(i):
        apart = lax.rem(i, 2) * (doms // 2) + lax.div(i, 2)
        if doms & (doms - 1):
            return lax.rem(my_dom + apart, doms)
        other, bit = 0, 1
        while bit < doms:
            differ = lax.rem(lax.div(my_dom, bit) + lax.div(apart, bit), 2)
            other, bit = other + differ * bit, bit * 2
        return other

    def send_packet(i, carry):
        dom = partner(i)
        packets[pl.ds(at(dom, chunk), chunk), :] = pick(dom)
        packet(dom).start()
        return carry

    lax.fori_loop(1, doms, send_packet, 0)
    received[pl.ds(at(my_dom, chunk), chunk), :] = pick(my_dom)

    lax.fori_loop(new_count // 32, new_count // 16, prepare_mass, 0)

    def prepare_cross(j, carry):
        pair_blocks(cross_ref, j, block)

        def cut(i, inner):
            cross[pl.ds(at(j * 8 + i, LANES), LANES), :] = jnp.transpose(
                block[pl.ds(at(i, LANES), LANES), :]
            ).astype(BF16)
            return inner

        return lax.fori_loop(0, 8, cut, carry, unroll=4)

    loads[2].wait()
    lax.fori_loop(0, slots // 16, prepare_cross, 0)

    def arrive(dom, carry):
        @pl.when(dom != my_dom)
        def _():
            pltpu.make_async_remote_copy(
                src_ref=packets.at[pl.ds(at(dom, chunk), chunk), :],
                dst_ref=received.at[pl.ds(at(dom, chunk), chunk), :],
                send_sem=packet_send.at[dom], recv_sem=packet_recv.at[dom],
                device_id={"slab": my_slab, "dom": dom}, device_id_type=pl.DeviceIdType.MESH,
            ).wait()

        return carry

    lax.fori_loop(0, doms, arrive, 0)

    senders = 16 // cap

    def product(step, carry):
        j, h = lax.div(step, senders // 2), lax.rem(step, senders // 2)
        first = received[pl.ds(at(j * senders + h, chunk), chunk), :].astype(F32)
        second = received[pl.ds(at(j * senders + senders // 2 + h, chunk), chunk), :].astype(F32)
        for c in range(cap):
            part = slice(c * HALF, (c + 1) * HALF)
            pair = j * 8 + h * cap + c
            field = jnp.concatenate(interleave(first[part], second[part]), axis=0).astype(BF16)
            matrix = cross[pl.ds(at(pair, LANES), LANES), :]
            contrib[pl.ds(at(pair, V), V), :] = jnp.dot(
                field, matrix, preferred_element_type=F32
            )
        return carry

    lax.fori_loop(0, doms // 2, product, 0, unroll=4)

    shape = (new_count, slots)
    onehot = jnp.where(lax.broadcasted_iota(jnp.int32, shape, 0) == target_ref[...], 1.0, 0.0).astype(BF16)
    pairs_in = slots // 2

    def scatter(t, carry):
        even = contrib[pl.ds(t, pairs_in, stride=V), :]
        odd = contrib[pl.ds(HALF + t, pairs_in, stride=V), :]
        first, second = interleave(even, odd)
        rows = []
        for j in range(pairs_in // 8):
            rows += [first[j * 8:j * 8 + 8], second[j * 8:j * 8 + 8]]
        terms = jnp.concatenate(split(jnp.concatenate(rows, axis=0)), axis=1)
        total = jnp.dot(onehot, terms, preferred_element_type=F32)
        total = total[:, :LANES] + total[:, LANES:]
        for j in range(new_count // 16):
            even, odd = interleave(total[j * 16:j * 16 + 8], total[j * 16 + 8:j * 16 + 16])
            residual[pl.ds(j * 8 * V + t, 8, stride=V), :] = even
            residual[pl.ds(j * 8 * V + HALF + t, 8, stride=V), :] = odd
        return carry

    lax.fori_loop(0, HALF, scatter, 0, unroll=6)

    pairs = new_count // 2

    def apply_mass(pair, field):
        terms = jnp.concatenate(split(field), axis=0)
        result = jnp.dot(terms, blocks[pl.ds(at(pair, LANES), LANES), :], preferred_element_type=F32)
        return (result[V:, :LANES] + result[:V, LANES:]) + result[:V, :LANES]

    def sum_start(step, parts):
        stack = jnp.sum(jnp.concatenate(parts, axis=0), axis=1, keepdims=True)
        half = stack.shape[0] // 2
        own = jnp.concatenate([column_to_row(stack[:half]), column_to_row(stack[half:])], axis=0)
        sums[step] = own

        def send(i, where):
            pltpu.make_async_remote_copy(
                src_ref=sums.at[step], dst_ref=sums_in.at[step, i],
                send_sem=sum_send.at[step], recv_sem=sum_recv.at[step],
                device_id=where, device_id_type=pl.DeviceIdType.MESH,
            ).start()

        each_device(send)
        return own

    def sum_end(step, own, count):
        arrived = sums_in.at[step, 0:devices - 1]
        pltpu.make_async_copy(arrived, arrived, sum_recv.at[step]).wait()
        total = own + jnp.sum(sums_in[step, 0:devices - 1], axis=0)
        half = count * V // 2
        column = jnp.concatenate([row_to_column(total[:1], half), row_to_column(total[1:], half)], axis=0)
        return [column[n * V:(n + 1) * V] for n in range(count)]

    zero = jnp.zeros((V, LANES), F32)
    small = jnp.zeros((HALF, LANES), F32)

    def first_pass(pair, carry):
        bb, bw, ww, wq = carry
        at_pair = pl.ds(at(pair, V), V)
        b = residual[at_pair, :]
        w = apply_mass(pair, b)
        image[at_pair, :] = w
        q = apply_mass(pair, w)
        image2[at_pair, :] = q
        return bb + b * b, bw + b * w, ww + w * w, wq + w * q

    own = sum_start(0, lax.fori_loop(0, pairs, first_pass, (zero,) * 4, unroll=8))

    def third_image(pair, carry):
        at_pair = pl.ds(at(pair, V), V)
        image3[at_pair, :] = apply_mass(pair, image2[at_pair, :])
        return carry

    lax.fori_loop(0, pairs, third_image, 0, unroll=8)
    bb, bw, ww, wq = sum_end(0, own, 4)

    alpha = bb / bw
    norm = alpha * (alpha * ww) - bb
    weighted = bw - 2.0 * (alpha * ww) + alpha * (alpha * wq)
    beta = norm / bb
    curve = weighted - beta * (norm / alpha)
    sound = jnp.logical_and(norm > FLOOR * bb, curve > 0.0)
    beta = jnp.where(sound, beta, 0.0)
    alpha1 = jnp.where(sound, norm / jnp.where(sound, curve, 1.0), alpha)

    dots = []
    for part in range(2):
        rows = slice(part * HALF, (part + 1) * HALF)
        a0, a1, grow = (
            jnp.broadcast_to(value[rows], (HALF, LANES)) for value in (alpha, alpha1, 1.0 + beta)
        )

        def second_pass(pair, carry, part=part, a0=a0, a1=a1, grow=grow):
            rr, rw, rs, ps, rp = carry
            at_pair = pl.ds(at(pair * 2 + part, HALF), HALF)
            b, w, q, t = (ref[at_pair, :] for ref in (residual, image, image2, image3))
            p = grow * b - a0 * w
            s = grow * w - a0 * q
            r = (b - a0 * w) - a1 * s
            v = (w - a0 * q) - a1 * (grow * q - a0 * t)
            image3[at_pair, :] = a0 * b + a1 * p
            image2[at_pair, :] = p
            residual[at_pair, :] = r
            return rr + r * r, rw + r * v, rs + r * s, ps + p * s, rp + r * p

        dots.append(lax.fori_loop(0, pairs, second_pass, (small,) * 5, unroll=4))

    own = sum_start(1, [half for pair in zip(*dots) for half in pair])

    def flatten(pair, carry):
        at_pair = pl.ds(at(pair, V), V)
        number = lax.div(pair, 8) * 16 + lax.rem(pair, 8)
        for src, dst in ((image3, flat_x), (image2, flat_p), (residual, flat_r)):
            value = src[at_pair, :]
            first, second = interleave(value[:HALF], value[HALF:])
            dst[pl.ds(at(number, HALF), HALF), :] = first
            dst[pl.ds(at(number + 8, HALF), HALF), :] = second
        return carry

    lax.fori_loop(0, pairs, flatten, 0, unroll=4)
    rr, rw, rs, ps, rp = sum_end(1, own, 5)
    beta = -rs / ps
    alpha = (rr + beta * rp) / (rw + beta * (2.0 * rs + beta * ps))

    def flat_factor(column):
        wide = jnp.broadcast_to(column, (V, LANES))
        return jnp.where(left_half((HALF, LANES)), wide[:HALF], wide[HALF:])

    factor_r = flat_factor(alpha)
    factor_p = flat_factor(alpha * beta)

    used = group * HALF

    def code(dom):
        rows = []
        for g in range(group):
            which = pl.ds(order_ref[0, dom * group + g] * HALF, HALF)
            rows.append(flat_x[which, :] + (factor_p * flat_p[which, :] + factor_r * flat_r[which, :]))
        value = jnp.concatenate(rows, axis=0)
        top = jnp.maximum(jnp.max(jnp.abs(value), axis=1, keepdims=True), 1e-30)
        coded = jnp.round(value * (LIMIT / top)).astype(jnp.int32)
        if code_rows > used:
            coded = jnp.concatenate([coded, jnp.zeros((code_rows - used, LANES), jnp.int32)], axis=0)
        return coded.astype(jnp.int16), column_to_row(top * (1.0 / LIMIT))

    def code_copies(to, frm, dst):
        where = {"slab": my_slab, "dom": to}
        return [
            pltpu.make_async_remote_copy(
                src_ref=codes.at[pl.ds(at(to, code_rows), code_rows), :],
                dst_ref=codes_in.at[pl.ds(at(dst, code_rows), code_rows), :],
                send_sem=code_send.at[to], recv_sem=code_recv.at[frm],
                device_id=where, device_id_type=pl.DeviceIdType.MESH,
            ),
            pltpu.make_async_remote_copy(
                src_ref=scales.at[pl.ds(to, 1), :], dst_ref=scales_in.at[pl.ds(dst, 1), :],
                send_sem=scale_send.at[to], recv_sem=scale_recv.at[frm],
                device_id=where, device_id_type=pl.DeviceIdType.MESH,
            ),
        ]

    def send_code(i, carry):
        dom = partner(i)
        coded, scale = code(dom)
        codes[pl.ds(at(dom, code_rows), code_rows), :] = coded
        scales[pl.ds(dom, 1), :] = scale
        for copy in code_copies(dom, my_dom, my_dom):
            copy.start()
        return carry

    lax.fori_loop(1, doms, send_code, 0)
    coded, scale = code(my_dom)

    codes_out[pl.ds(at(my_dom, code_rows), code_rows), :] = coded
    scales_out[pl.ds(my_dom, 1), :] = scale

    def take(dom, carry):
        @pl.when(dom != my_dom)
        def _():
            for copy in code_copies(dom, dom, dom):
                copy.wait()
            here = pl.ds(at(dom, code_rows), code_rows)
            codes_out[here, :] = codes_in[here, :]
            scales_out[pl.ds(dom, 1), :] = scales_in[pl.ds(dom, 1), :]

        return carry

    lax.fori_loop(0, doms, take, 0)

    for step in range(SUMS):
        left = sums_in.at[step, 0:devices - 1]
        pltpu.make_async_copy(left, left, sum_send.at[step]).wait()

    @pl.when(my_slab < slabs - 1)
    def _():
        up.wait_send()

    @pl.when(my_slab > 0)
    def _():
        down.wait_send()


def unfold_kernel(used, code_rows, codes_ref, scales_ref, dst, placed, held, store_sem):
    senders = 8 * HALF // used
    stores = []
    for block in range(held.shape[0] // 8):
        for n in range(senders):
            dom = block * senders + n
            value = codes_ref[dom * code_rows:(dom + 1) * code_rows, :].astype(jnp.int32).astype(F32)[:used]
            scale = row_to_column(scales_ref[dom:dom + 1, :], used)
            row = (block * senders + n) * used
            placed[row:row + used, :] = value * scale
        part = slice(block * 8, (block + 1) * 8)
        for t in range(HALF):
            held[part, t * LANES:(t + 1) * LANES] = placed[pl.ds(block * 8 * HALF + t, 8, stride=HALF), :]
        store = pltpu.make_async_copy(held.at[part, :], dst.at[part, :], store_sem.at[block])
        store.start()
        stores.append(store)
    for store in stores:
        store.wait()


def unfold(codes, scales, new_count, used, code_rows):
    shape = (new_count, V * Q)
    return pl.pallas_call(
        functools.partial(unfold_kernel, used, code_rows),
        out_shape=jax.ShapeDtypeStruct(shape, F32),
        in_specs=[pl.BlockSpec(memory_space=pltpu.VMEM)] * 2,
        out_specs=pl.BlockSpec(memory_space=pl.ANY),
        scratch_shapes=[
            pltpu.VMEM((new_count * HALF, LANES), F32),
            pltpu.VMEM(shape, F32),
            pltpu.SemaphoreType.DMA((new_count // 8,)),
        ],
        compiler_params=pltpu.CompilerParams(vmem_limit_bytes=56 * 1024 * 1024),
    )(codes, scales)


def per_device(slabs, doms, state, send_index, send_count, slot_target, cross_mass, mass, new_order):
    cap = send_index.shape[3]
    new_count = mass.shape[1]
    group = new_count // doms
    slots = doms * cap
    pool_rows = (state.shape[1] + 2 * RIM) * HALF
    rim_rows = RIM * HALF
    code_rows = -(-group * HALF // 16) * 16
    devices = slabs * doms
    steps = SUMS
    vmem, smem = pltpu.VMEM, pltpu.SMEM
    dma = pltpu.SemaphoreType.DMA
    field = vmem((new_count * HALF, LANES), F32)
    scratch = [
        vmem(state.shape[1:], BF16),
        vmem((slots, Q * Q), BF16),
        vmem((new_count, Q * Q), F32),
        dma((3,)),
        vmem((pool_rows, LANES), F32),
        *[vmem((rim_rows, LANES), BF16)] * 4,
        vmem((slots * HALF, LANES), BF16),
        vmem((slots * HALF, LANES), BF16),
        vmem((8 * LANES, LANES), F32),
        vmem((slots // 2 * LANES, LANES), BF16),
        vmem((new_count // 2 * LANES, 2 * LANES), BF16),
        vmem((slots * HALF, LANES), F32),
        *[field] * 7,
        vmem((doms * code_rows, LANES), jnp.int16),
        vmem((doms * code_rows, LANES), jnp.int16),
        vmem((doms, LANES), F32),
        vmem((doms, LANES), F32),
        vmem((steps, 2, LANES), F32),
        vmem((steps, devices, 2, LANES), F32),
        dma((2,)), dma((2,)), dma((doms,)), dma((doms,)),
        dma((steps,)), dma((steps,)),
        dma((doms,)), dma((doms,)), dma((doms,)), dma((doms,)),
    ]
    codes, scales = pl.pallas_call(
        functools.partial(kernel, slabs, doms, cap, group),
        out_shape=(
            jax.ShapeDtypeStruct((doms * code_rows, LANES), jnp.int16),
            jax.ShapeDtypeStruct((doms, LANES), F32),
        ),
        in_specs=[pl.BlockSpec(memory_space=smem)] * 3 + [pl.BlockSpec(memory_space=vmem)]
        + [pl.BlockSpec(memory_space=pltpu.HBM)] * 3,
        out_specs=[pl.BlockSpec(memory_space=vmem)] * 2,
        scratch_shapes=scratch,
        compiler_params=pltpu.CompilerParams(
            collective_id=0, has_side_effects=True, vmem_limit_bytes=56 * 1024 * 1024
        ),
        cost_estimate=pl.CostEstimate(flops=10**9, bytes_accessed=4 * 10**6, transcendentals=0),
    )(
        send_index[0, 0].T, send_count[0], new_order[0], slot_target[0],
        state[0], cross_mass[0, 0], mass[0],
    )
    return unfold(codes, scales, new_count, group * HALF, code_rows)[None]


def solution(mesh):
    in_specs = (
        P("dom", "slab", None),
        P("dom", "slab", None, None),
        P("dom", "slab", None),
        P("dom", "slab", None),
        P("dom", "slab", None, None),
        P("dom", "slab", None),
        P("dom", "slab", None),
    )
    return jax.shard_map(
        functools.partial(per_device, mesh.shape["slab"], mesh.shape["dom"]),
        mesh=mesh, in_specs=in_specs, out_specs=P("dom", "slab", None), check_vma=False,
    )
```

```python
import functools

import jax
import jax.numpy as jnp
from jax import lax
from jax.experimental import pallas as pl
from jax.experimental.pallas import tpu as pltpu
from jax.sharding import PartitionSpec as P

Q = 64
V = 48
RIM = 8
LANES = 128
HALF = V // 2
SUMS = 2
FLOOR = 1e-4
F32 = jnp.float32
BF16 = jnp.bfloat16
LIMIT = 32767.0


def at(index, unit):
    return pl.multiple_of(index * unit, unit)


def left_half(shape):
    return lax.broadcasted_iota(jnp.int32, shape, 1) < Q


def swap(value):
    return pltpu.roll(value, Q, 1)


def interleave(first, second):
    left = left_half(first.shape)
    return jnp.where(left, first, swap(second)), jnp.where(left, swap(first), second)


def split(value):
    high = value.astype(BF16)
    return high, (value - high.astype(F32)).astype(BF16)


def eye(rows):
    shape = (rows, LANES)
    return lax.broadcasted_iota(jnp.int32, shape, 0) == lax.broadcasted_iota(jnp.int32, shape, 1)


def column_to_row(column):
    spread = jnp.where(eye(column.shape[0]), column, 0.0)
    return jnp.sum(spread, axis=0, keepdims=True)


def row_to_column(row, rows):
    spread = jnp.where(eye(rows), row, 0.0)
    return jnp.sum(spread, axis=1, keepdims=True)


def pair_blocks(source, group, block):
    left = left_half((8, LANES))

    def body(t, carry):
        both = source[pl.ds(at(group, 16), 16), pl.ds(at(t, LANES), LANES)].astype(F32)
        first, second = both[:8], both[8:]
        block[pl.ds(2 * t, 8, stride=LANES), :] = jnp.where(left, first, 0.0)
        block[pl.ds(2 * t + 1, 8, stride=LANES), :] = jnp.where(left, swap(first), 0.0)
        block[pl.ds(Q + 2 * t, 8, stride=LANES), :] = jnp.where(left, 0.0, swap(second))
        block[pl.ds(Q + 2 * t + 1, 8, stride=LANES), :] = jnp.where(left, 0.0, second)
        return carry

    lax.fori_loop(0, Q // 2, body, 0, unroll=8)


def kernel(
    slabs, doms, cap, group,
    index_ref, count_ref, order_ref, target_ref, state_hbm, cross_hbm, mass_hbm,
    codes_out, scales_out,
    state_ref, cross_ref, mass_ref, load_sem,
    pool, up_out, down_out, up_in, down_in, packets, received, block, cross, blocks,
    contrib, residual, image, image2, image3, flat_x, flat_p, flat_r, codes, codes_in, scales, scales_in,
    sums, sums_in,
    halo_send, halo_recv, packet_send, packet_recv, sum_send, sum_recv,
    code_send, code_recv, scale_send, scale_recv,
):
    my_slab, my_dom = lax.axis_index("slab"), lax.axis_index("dom")
    devices = slabs * doms
    elements = state_ref.shape[0]
    slots = cross_ref.shape[0]
    new_count = mass_ref.shape[0]
    chunk = cap * HALF
    code_rows = codes.shape[0] // doms

    def wrap(value, size):
        return jnp.where(value >= size, value - size, value)

    def each_device(act):
        for apart in range(slabs):
            slab = wrap(my_slab + apart, slabs)

            def body(i, carry, apart=apart, slab=slab):
                act(apart * doms + i - 1, {"slab": slab, "dom": wrap(my_dom + i, doms)})
                return carry

            lax.fori_loop(1 if apart == 0 else 0, doms, body, 0, unroll=3 if apart == 0 else 4)

    loads = [
        pltpu.make_async_copy(src, dst, load_sem.at[n])
        for n, (src, dst) in enumerate(
            ((state_hbm, state_ref), (mass_hbm, mass_ref), (cross_hbm, cross_ref))
        )
    ]
    for load in loads:
        load.start()
    barrier = pltpu.get_barrier_semaphore()

    def greet(i, where):
        pl.semaphore_signal(barrier, inc=1, device_id=where, device_id_type=pl.DeviceIdType.MESH)

    each_device(greet)

    loads[0].wait()

    def unfold(t, carry):
        for row in range(0, elements, 16):
            part = state_ref[row:row + 16, pl.ds(at(t, LANES), LANES)].astype(F32)
            pool[pl.ds((RIM + row) * HALF + t, 8, stride=HALF), :] = part[:8]
            pool[pl.ds((RIM + row + 8) * HALF + t, 8, stride=HALF), :] = part[8:]
        return carry

    lax.fori_loop(0, HALF, unfold, 0, unroll=4)
    rim_rows = RIM * HALF
    last = (RIM + elements) * HALF
    down_out[...] = pool[rim_rows:2 * rim_rows, :].astype(BF16)
    up_out[...] = pool[last - rim_rows:last, :].astype(BF16)
    pl.semaphore_wait(barrier, devices - 1)

    def halo(which, src, dst, slab):
        return pltpu.make_async_remote_copy(
            src_ref=src, dst_ref=dst, send_sem=halo_send.at[which], recv_sem=halo_recv.at[which],
            device_id={"slab": slab, "dom": my_dom}, device_id_type=pl.DeviceIdType.MESH,
        )

    up = halo(0, up_out, up_in, lax.rem(my_slab + 1, slabs))
    down = halo(1, down_out, down_in, lax.rem(my_slab + slabs - 1, slabs))

    @pl.when(my_slab < slabs - 1)
    def _():
        up.start()

    @pl.when(my_slab > 0)
    def _():
        down.start()

    loads[1].wait()

    def prepare_mass(j, carry):
        pair_blocks(mass_ref, j, block)

        def cut(i, inner):
            high, low = split(block[pl.ds(at(i, LANES), LANES), :])
            blocks[pl.ds(at(j * 8 + i, LANES), LANES), 0:LANES] = high
            blocks[pl.ds(at(j * 8 + i, LANES), LANES), LANES:2 * LANES] = low
            return inner

        return lax.fori_loop(0, 8, cut, carry, unroll=4)

    lax.fori_loop(0, new_count // 32, prepare_mass, 0)

    @pl.when(my_slab > 0)
    def _():
        up.wait_recv()
        pool[0:rim_rows, :] = up_in[...].astype(F32)

    @pl.when(my_slab == 0)
    def _():
        pool[0:rim_rows, :] = jnp.zeros((rim_rows, LANES), F32)

    @pl.when(my_slab < slabs - 1)
    def _():
        down.wait_recv()
        pool[last:last + rim_rows, :] = down_in[...].astype(F32)

    @pl.when(my_slab == slabs - 1)
    def _():
        pool[last:last + rim_rows, :] = jnp.zeros((rim_rows, LANES), F32)

    def pick(dom):
        live = count_ref[0, dom]
        rows = []
        for c in range(cap):
            row = pool[pl.ds(index_ref[c, dom] * HALF, HALF), :]
            rows.append(row * jnp.minimum(jnp.maximum(live - c, 0), 1).astype(F32))
        return jnp.concatenate(rows, axis=0).astype(BF16)

    def packet(dom):
        return pltpu.make_async_remote_copy(
            src_ref=packets.at[pl.ds(at(dom, chunk), chunk), :],
            dst_ref=received.at[pl.ds(at(my_dom, chunk), chunk), :],
            send_sem=packet_send.at[dom], recv_sem=packet_recv.at[my_dom],
            device_id={"slab": my_slab, "dom": dom}, device_id_type=pl.DeviceIdType.MESH,
        )

    def partner(i):
        apart = lax.rem(i, 2) * (doms // 2) + lax.div(i, 2)
        if doms & (doms - 1):
            return lax.rem(my_dom + apart, doms)
        other, bit = 0, 1
        while bit < doms:
            differ = lax.rem(lax.div(my_dom, bit) + lax.div(apart, bit), 2)
            other, bit = other + differ * bit, bit * 2
        return other

    def send_packet(i, carry):
        dom = partner(i)
        packets[pl.ds(at(dom, chunk), chunk), :] = pick(dom)
        packet(dom).start()
        return carry

    lax.fori_loop(1, doms, send_packet, 0)
    received[pl.ds(at(my_dom, chunk), chunk), :] = pick(my_dom)

    lax.fori_loop(new_count // 32, new_count // 16, prepare_mass, 0)

    def prepare_cross(j, carry):
        pair_blocks(cross_ref, j, block)

        def cut(i, inner):
            cross[pl.ds(at(j * 8 + i, LANES), LANES), :] = jnp.transpose(
                block[pl.ds(at(i, LANES), LANES), :]
            ).astype(BF16)
            return inner

        return lax.fori_loop(0, 8, cut, carry, unroll=4)

    loads[2].wait()
    lax.fori_loop(0, slots // 16, prepare_cross, 0)

    def arrive(dom, carry):
        @pl.when(dom != my_dom)
        def _():
            pltpu.make_async_remote_copy(
                src_ref=packets.at[pl.ds(at(dom, chunk), chunk), :],
                dst_ref=received.at[pl.ds(at(dom, chunk), chunk), :],
                send_sem=packet_send.at[dom], recv_sem=packet_recv.at[dom],
                device_id={"slab": my_slab, "dom": dom}, device_id_type=pl.DeviceIdType.MESH,
            ).wait()

        return carry

    senders = 16 // cap

    def product(step, carry):
        j, h = lax.div(step, senders // 2), lax.rem(step, senders // 2)
        first = received[pl.ds(at(j * senders + h, chunk), chunk), :].astype(F32)
        second = received[pl.ds(at(j * senders + senders // 2 + h, chunk), chunk), :].astype(F32)
        for c in range(cap):
            part = slice(c * HALF, (c + 1) * HALF)
            pair = j * 8 + h * cap + c
            field = jnp.concatenate(interleave(first[part], second[part]), axis=0).astype(BF16)
            matrix = cross[pl.ds(at(pair, LANES), LANES), :]
            contrib[pl.ds(at(pair, V), V), :] = jnp.dot(
                field, matrix, preferred_element_type=F32
            )
        return carry

    own_half = jnp.where(my_dom >= doms // 2, 1, 0)
    for half in (own_half, 1 - own_half):
        lax.fori_loop(0, doms // 2, lambda n, c, half=half: arrive(half * (doms // 2) + n, c), 0)
        lax.fori_loop(0, doms // 4, lambda n, c, half=half: product(half * (doms // 4) + n, c), 0, unroll=4)

    shape = (new_count, slots)
    onehot = jnp.where(lax.broadcasted_iota(jnp.int32, shape, 0) == target_ref[...], 1.0, 0.0).astype(BF16)
    pairs_in = slots // 2

    def scatter(t, carry):
        even = contrib[pl.ds(t, pairs_in, stride=V), :]
        odd = contrib[pl.ds(HALF + t, pairs_in, stride=V), :]
        first, second = interleave(even, odd)
        rows = []
        for j in range(pairs_in // 8):
            rows += [first[j * 8:j * 8 + 8], second[j * 8:j * 8 + 8]]
        terms = jnp.concatenate(split(jnp.concatenate(rows, axis=0)), axis=1)
        total = jnp.dot(onehot, terms, preferred_element_type=F32)
        total = total[:, :LANES] + total[:, LANES:]
        for j in range(new_count // 16):
            even, odd = interleave(total[j * 16:j * 16 + 8], total[j * 16 + 8:j * 16 + 16])
            residual[pl.ds(j * 8 * V + t, 8, stride=V), :] = even
            residual[pl.ds(j * 8 * V + HALF + t, 8, stride=V), :] = odd
        return carry

    lax.fori_loop(0, HALF, scatter, 0, unroll=6)

    pairs = new_count // 2

    def apply_mass(pair, field):
        terms = jnp.concatenate(split(field), axis=0)
        result = jnp.dot(terms, blocks[pl.ds(at(pair, LANES), LANES), :], preferred_element_type=F32)
        return (result[V:, :LANES] + result[:V, LANES:]) + result[:V, :LANES]

    def sum_start(step, parts):
        stack = jnp.sum(jnp.concatenate(parts, axis=0), axis=1, keepdims=True)
        half = stack.shape[0] // 2
        own = jnp.concatenate([column_to_row(stack[:half]), column_to_row(stack[half:])], axis=0)
        sums[step] = own

        def send(i, where):
            pltpu.make_async_remote_copy(
                src_ref=sums.at[step], dst_ref=sums_in.at[step, i],
                send_sem=sum_send.at[step], recv_sem=sum_recv.at[step],
                device_id=where, device_id_type=pl.DeviceIdType.MESH,
            ).start()

        each_device(send)
        return own

    def sum_end(step, own, count):
        arrived = sums_in.at[step, 0:devices - 1]
        pltpu.make_async_copy(arrived, arrived, sum_recv.at[step]).wait()
        total = own + jnp.sum(sums_in[step, 0:devices - 1], axis=0)
        half = count * V // 2
        column = jnp.concatenate([row_to_column(total[:1], half), row_to_column(total[1:], half)], axis=0)
        return [column[n * V:(n + 1) * V] for n in range(count)]

    zero = jnp.zeros((V, LANES), F32)
    small = jnp.zeros((HALF, LANES), F32)

    def first_pass(pair, carry):
        bb, bw, ww, wq = carry
        at_pair = pl.ds(at(pair, V), V)
        b = residual[at_pair, :]
        w = apply_mass(pair, b)
        image[at_pair, :] = w
        q = apply_mass(pair, w)
        image2[at_pair, :] = q
        return bb + b * b, bw + b * w, ww + w * w, wq + w * q

    own = sum_start(0, lax.fori_loop(0, pairs, first_pass, (zero,) * 4, unroll=8))

    def third_image(pair, carry):
        at_pair = pl.ds(at(pair, V), V)
        image3[at_pair, :] = apply_mass(pair, image2[at_pair, :])
        return carry

    lax.fori_loop(0, pairs, third_image, 0, unroll=8)
    bb, bw, ww, wq = sum_end(0, own, 4)

    alpha = bb / bw
    norm = alpha * (alpha * ww) - bb
    weighted = bw - 2.0 * (alpha * ww) + alpha * (alpha * wq)
    beta = norm / bb
    curve = weighted - beta * (norm / alpha)
    sound = jnp.logical_and(norm > FLOOR * bb, curve > 0.0)
    beta = jnp.where(sound, beta, 0.0)
    alpha1 = jnp.where(sound, norm / jnp.where(sound, curve, 1.0), alpha)

    dots = []
    for part in range(2):
        rows = slice(part * HALF, (part + 1) * HALF)
        a0, a1, grow = (
            jnp.broadcast_to(value[rows], (HALF, LANES)) for value in (alpha, alpha1, 1.0 + beta)
        )

        def second_pass(pair, carry, part=part, a0=a0, a1=a1, grow=grow):
            rr, rw, rs, ps, rp = carry
            at_pair = pl.ds(at(pair * 2 + part, HALF), HALF)
            b, w, q, t = (ref[at_pair, :] for ref in (residual, image, image2, image3))
            p = grow * b - a0 * w
            s = grow * w - a0 * q
            r = (b - a0 * w) - a1 * s
            v = (w - a0 * q) - a1 * (grow * q - a0 * t)
            image3[at_pair, :] = a0 * b + a1 * p
            image2[at_pair, :] = p
            residual[at_pair, :] = r
            return rr + r * r, rw + r * v, rs + r * s, ps + p * s, rp + r * p

        dots.append(lax.fori_loop(0, pairs, second_pass, (small,) * 5, unroll=4))

    own = sum_start(1, [half for pair in zip(*dots) for half in pair])

    def flatten(pair, carry):
        at_pair = pl.ds(at(pair, V), V)
        number = lax.div(pair, 8) * 16 + lax.rem(pair, 8)
        for src, dst in ((image3, flat_x), (image2, flat_p), (residual, flat_r)):
            value = src[at_pair, :]
            first, second = interleave(value[:HALF], value[HALF:])
            dst[pl.ds(at(number, HALF), HALF), :] = first
            dst[pl.ds(at(number + 8, HALF), HALF), :] = second
        return carry

    lax.fori_loop(0, pairs, flatten, 0, unroll=4)
    rr, rw, rs, ps, rp = sum_end(1, own, 5)
    beta = -rs / ps
    alpha = (rr + beta * rp) / (rw + beta * (2.0 * rs + beta * ps))

    def flat_factor(column):
        wide = jnp.broadcast_to(column, (V, LANES))
        return jnp.where(left_half((HALF, LANES)), wide[:HALF], wide[HALF:])

    factor_r = flat_factor(alpha)
    factor_p = flat_factor(alpha * beta)

    used = group * HALF

    def code(dom):
        rows = []
        for g in range(group):
            which = pl.ds(order_ref[0, dom * group + g] * HALF, HALF)
            rows.append(flat_x[which, :] + (factor_p * flat_p[which, :] + factor_r * flat_r[which, :]))
        value = jnp.concatenate(rows, axis=0)
        top = jnp.maximum(jnp.max(jnp.abs(value), axis=1, keepdims=True), 1e-30)
        coded = jnp.round(value * (LIMIT / top)).astype(jnp.int32)
        if code_rows > used:
            coded = jnp.concatenate([coded, jnp.zeros((code_rows - used, LANES), jnp.int32)], axis=0)
        return coded.astype(jnp.int16), column_to_row(top * (1.0 / LIMIT))

    def code_copies(to, frm, dst):
        where = {"slab": my_slab, "dom": to}
        return [
            pltpu.make_async_remote_copy(
                src_ref=codes.at[pl.ds(at(to, code_rows), code_rows), :],
                dst_ref=codes_in.at[pl.ds(at(dst, code_rows), code_rows), :],
                send_sem=code_send.at[to], recv_sem=code_recv.at[frm],
                device_id=where, device_id_type=pl.DeviceIdType.MESH,
            ),
            pltpu.make_async_remote_copy(
                src_ref=scales.at[pl.ds(to, 1), :], dst_ref=scales_in.at[pl.ds(dst, 1), :],
                send_sem=scale_send.at[to], recv_sem=scale_recv.at[frm],
                device_id=where, device_id_type=pl.DeviceIdType.MESH,
            ),
        ]

    def send_code(i, carry):
        dom = partner(i)
        coded, scale = code(dom)
        codes[pl.ds(at(dom, code_rows), code_rows), :] = coded
        scales[pl.ds(dom, 1), :] = scale
        for copy in code_copies(dom, my_dom, my_dom):
            copy.start()
        return carry

    lax.fori_loop(1, doms, send_code, 0)
    coded, scale = code(my_dom)

    codes_out[pl.ds(at(my_dom, code_rows), code_rows), :] = coded
    scales_out[pl.ds(my_dom, 1), :] = scale

    def take(dom, carry):
        @pl.when(dom != my_dom)
        def _():
            for copy in code_copies(dom, dom, dom):
                copy.wait()
            here = pl.ds(at(dom, code_rows), code_rows)
            codes_out[here, :] = codes_in[here, :]
            scales_out[pl.ds(dom, 1), :] = scales_in[pl.ds(dom, 1), :]

        return carry

    lax.fori_loop(0, doms, take, 0)

    for step in range(SUMS):
        left = sums_in.at[step, 0:devices - 1]
        pltpu.make_async_copy(left, left, sum_send.at[step]).wait()

    @pl.when(my_slab < slabs - 1)
    def _():
        up.wait_send()

    @pl.when(my_slab > 0)
    def _():
        down.wait_send()


def unfold_kernel(used, code_rows, codes_ref, scales_ref, dst, placed, held, store_sem):
    senders = 8 * HALF // used
    stores = []
    for block in range(held.shape[0] // 8):
        for n in range(senders):
            dom = block * senders + n
            value = codes_ref[dom * code_rows:(dom + 1) * code_rows, :].astype(jnp.int32).astype(F32)[:used]
            scale = row_to_column(scales_ref[dom:dom + 1, :], used)
            row = (block * senders + n) * used
            placed[row:row + used, :] = value * scale
        part = slice(block * 8, (block + 1) * 8)
        for t in range(HALF):
            held[part, t * LANES:(t + 1) * LANES] = placed[pl.ds(block * 8 * HALF + t, 8, stride=HALF), :]
        store = pltpu.make_async_copy(held.at[part, :], dst.at[part, :], store_sem.at[block])
        store.start()
        stores.append(store)
    for store in stores:
        store.wait()


def unfold(codes, scales, new_count, used, code_rows):
    shape = (new_count, V * Q)
    return pl.pallas_call(
        functools.partial(unfold_kernel, used, code_rows),
        out_shape=jax.ShapeDtypeStruct(shape, F32),
        in_specs=[pl.BlockSpec(memory_space=pltpu.VMEM)] * 2,
        out_specs=pl.BlockSpec(memory_space=pl.ANY),
        scratch_shapes=[
            pltpu.VMEM((new_count * HALF, LANES), F32),
            pltpu.VMEM(shape, F32),
            pltpu.SemaphoreType.DMA((new_count // 8,)),
        ],
        compiler_params=pltpu.CompilerParams(vmem_limit_bytes=56 * 1024 * 1024),
    )(codes, scales)


def per_device(slabs, doms, state, send_index, send_count, slot_target, cross_mass, mass, new_order):
    cap = send_index.shape[3]
    new_count = mass.shape[1]
    group = new_count // doms
    slots = doms * cap
    pool_rows = (state.shape[1] + 2 * RIM) * HALF
    rim_rows = RIM * HALF
    code_rows = -(-group * HALF // 16) * 16
    devices = slabs * doms
    steps = SUMS
    vmem, smem = pltpu.VMEM, pltpu.SMEM
    dma = pltpu.SemaphoreType.DMA
    field = vmem((new_count * HALF, LANES), F32)
    scratch = [
        vmem(state.shape[1:], BF16),
        vmem((slots, Q * Q), BF16),
        vmem((new_count, Q * Q), F32),
        dma((3,)),
        vmem((pool_rows, LANES), F32),
        *[vmem((rim_rows, LANES), BF16)] * 4,
        vmem((slots * HALF, LANES), BF16),
        vmem((slots * HALF, LANES), BF16),
        vmem((8 * LANES, LANES), F32),
        vmem((slots // 2 * LANES, LANES), BF16),
        vmem((new_count // 2 * LANES, 2 * LANES), BF16),
        vmem((slots * HALF, LANES), F32),
        *[field] * 7,
        vmem((doms * code_rows, LANES), jnp.int16),
        vmem((doms * code_rows, LANES), jnp.int16),
        vmem((doms, LANES), F32),
        vmem((doms, LANES), F32),
        vmem((steps, 2, LANES), F32),
        vmem((steps, devices, 2, LANES), F32),
        dma((2,)), dma((2,)), dma((doms,)), dma((doms,)),
        dma((steps,)), dma((steps,)),
        dma((doms,)), dma((doms,)), dma((doms,)), dma((doms,)),
    ]
    codes, scales = pl.pallas_call(
        functools.partial(kernel, slabs, doms, cap, group),
        out_shape=(
            jax.ShapeDtypeStruct((doms * code_rows, LANES), jnp.int16),
            jax.ShapeDtypeStruct((doms, LANES), F32),
        ),
        in_specs=[pl.BlockSpec(memory_space=smem)] * 3 + [pl.BlockSpec(memory_space=vmem)]
        + [pl.BlockSpec(memory_space=pltpu.HBM)] * 3,
        out_specs=[pl.BlockSpec(memory_space=vmem)] * 2,
        scratch_shapes=scratch,
        compiler_params=pltpu.CompilerParams(
            collective_id=0, has_side_effects=True, vmem_limit_bytes=56 * 1024 * 1024
        ),
        cost_estimate=pl.CostEstimate(flops=10**9, bytes_accessed=4 * 10**6, transcendentals=0),
    )(
        send_index[0, 0].T, send_count[0], new_order[0], slot_target[0],
        state[0], cross_mass[0, 0], mass[0],
    )
    return unfold(codes, scales, new_count, group * HALF, code_rows)[None]


def solution(mesh):
    in_specs = (
        P("dom", "slab", None),
        P("dom", "slab", None, None),
        P("dom", "slab", None),
        P("dom", "slab", None),
        P("dom", "slab", None, None),
        P("dom", "slab", None),
        P("dom", "slab", None),
    )
    return jax.shard_map(
        functools.partial(per_device, mesh.shape["slab"], mesh.shape["dom"]),
        mesh=mesh, in_specs=in_specs, out_specs=P("dom", "slab", None), check_vma=False,
    )
```

```python
import functools

import jax
import jax.numpy as jnp
from jax import lax
from jax.experimental import pallas as pl
from jax.experimental.pallas import tpu as pltpu
from jax.sharding import PartitionSpec as P

Q = 64
V = 48
RIM = 8
LANES = 128
HALF = V // 2
SUMS = 2
FLOOR = 1e-4
F32 = jnp.float32
BF16 = jnp.bfloat16
LIMIT = 32767.0


def at(index, unit):
    return pl.multiple_of(index * unit, unit)


def left_half(shape):
    return lax.broadcasted_iota(jnp.int32, shape, 1) < Q


def swap(value):
    return pltpu.roll(value, Q, 1)


def interleave(first, second):
    left = left_half(first.shape)
    return jnp.where(left, first, swap(second)), jnp.where(left, swap(first), second)


def split(value):
    high = value.astype(BF16)
    return high, (value - high.astype(F32)).astype(BF16)


def eye(rows):
    shape = (rows, LANES)
    return lax.broadcasted_iota(jnp.int32, shape, 0) == lax.broadcasted_iota(jnp.int32, shape, 1)


def column_to_row(column):
    spread = jnp.where(eye(column.shape[0]), column, 0.0)
    return jnp.sum(spread, axis=0, keepdims=True)


def row_to_column(row, rows):
    spread = jnp.where(eye(rows), row, 0.0)
    return jnp.sum(spread, axis=1, keepdims=True)


def pair_blocks(source, group, block):
    left = left_half((8, LANES))

    def body(t, carry):
        both = source[pl.ds(at(group, 16), 16), pl.ds(at(t, LANES), LANES)].astype(F32)
        first, second = both[:8], both[8:]
        block[pl.ds(2 * t, 8, stride=LANES), :] = jnp.where(left, first, 0.0)
        block[pl.ds(2 * t + 1, 8, stride=LANES), :] = jnp.where(left, swap(first), 0.0)
        block[pl.ds(Q + 2 * t, 8, stride=LANES), :] = jnp.where(left, 0.0, swap(second))
        block[pl.ds(Q + 2 * t + 1, 8, stride=LANES), :] = jnp.where(left, 0.0, second)
        return carry

    lax.fori_loop(0, Q // 2, body, 0, unroll=8)


def kernel(
    slabs, doms, cap, group,
    index_ref, count_ref, order_ref, target_ref, state_hbm, cross_hbm, mass_hbm,
    codes_out, scales_out,
    state_ref, cross_ref, mass_ref, load_sem,
    pool, up_out, down_out, up_in, down_in, packets, received, block, cross, blocks,
    contrib, residual, image, image2, image3, flat_x, flat_p, flat_r, codes, codes_in, scales, scales_in,
    sums, sums_in,
    halo_send, halo_recv, packet_send, packet_recv, sum_send, sum_recv,
    code_send, code_recv, scale_send, scale_recv,
):
    my_slab, my_dom = lax.axis_index("slab"), lax.axis_index("dom")
    devices = slabs * doms
    elements = state_ref.shape[0]
    slots = cross_ref.shape[0]
    new_count = mass_ref.shape[0]
    chunk = cap * HALF
    code_rows = codes.shape[0] // doms

    def wrap(value, size):
        return jnp.where(value >= size, value - size, value)

    def each_device(act):
        for apart in range(slabs):
            slab = wrap(my_slab + apart, slabs)

            def body(i, carry, apart=apart, slab=slab):
                act(apart * doms + i - 1, {"slab": slab, "dom": wrap(my_dom + i, doms)})
                return carry

            lax.fori_loop(1 if apart == 0 else 0, doms, body, 0, unroll=3 if apart == 0 else 4)

    loads = [
        pltpu.make_async_copy(src, dst, load_sem.at[n])
        for n, (src, dst) in enumerate(
            ((state_hbm, state_ref), (mass_hbm, mass_ref), (cross_hbm, cross_ref))
        )
    ]
    for load in loads:
        load.start()
    barrier = pltpu.get_barrier_semaphore()

    def greet(i, where):
        pl.semaphore_signal(barrier, inc=1, device_id=where, device_id_type=pl.DeviceIdType.MESH)

    each_device(greet)

    loads[0].wait()

    def unfold(t, carry):
        for row in range(0, elements, 16):
            part = state_ref[row:row + 16, pl.ds(at(t, LANES), LANES)].astype(F32)
            pool[pl.ds((RIM + row) * HALF + t, 8, stride=HALF), :] = part[:8]
            pool[pl.ds((RIM + row + 8) * HALF + t, 8, stride=HALF), :] = part[8:]
        return carry

    lax.fori_loop(0, HALF, unfold, 0, unroll=4)
    rim_rows = RIM * HALF
    last = (RIM + elements) * HALF
    down_out[...] = pool[rim_rows:2 * rim_rows, :].astype(BF16)
    up_out[...] = pool[last - rim_rows:last, :].astype(BF16)
    pl.semaphore_wait(barrier, devices - 1)

    def halo(which, src, dst, slab):
        return pltpu.make_async_remote_copy(
            src_ref=src, dst_ref=dst, send_sem=halo_send.at[which], recv_sem=halo_recv.at[which],
            device_id={"slab": slab, "dom": my_dom}, device_id_type=pl.DeviceIdType.MESH,
        )

    up = halo(0, up_out, up_in, lax.rem(my_slab + 1, slabs))
    down = halo(1, down_out, down_in, lax.rem(my_slab + slabs - 1, slabs))

    @pl.when(my_slab < slabs - 1)
    def _():
        up.start()

    @pl.when(my_slab > 0)
    def _():
        down.start()

    loads[1].wait()

    def prepare_mass(j, carry):
        pair_blocks(mass_ref, j, block)

        def cut(i, inner):
            high, low = split(block[pl.ds(at(i, LANES), LANES), :])
            blocks[pl.ds(at(j * 8 + i, LANES), LANES), 0:LANES] = high
            blocks[pl.ds(at(j * 8 + i, LANES), LANES), LANES:2 * LANES] = low
            return inner

        return lax.fori_loop(0, 8, cut, carry, unroll=4)

    lax.fori_loop(0, new_count // 32, prepare_mass, 0)

    @pl.when(my_slab > 0)
    def _():
        up.wait_recv()
        pool[0:rim_rows, :] = up_in[...].astype(F32)

    @pl.when(my_slab == 0)
    def _():
        pool[0:rim_rows, :] = jnp.zeros((rim_rows, LANES), F32)

    @pl.when(my_slab < slabs - 1)
    def _():
        down.wait_recv()
        pool[last:last + rim_rows, :] = down_in[...].astype(F32)

    @pl.when(my_slab == slabs - 1)
    def _():
        pool[last:last + rim_rows, :] = jnp.zeros((rim_rows, LANES), F32)

    def pick(dom):
        live = count_ref[0, dom]
        rows = []
        for c in range(cap):
            row = pool[pl.ds(index_ref[c, dom] * HALF, HALF), :]
            rows.append(row * jnp.minimum(jnp.maximum(live - c, 0), 1).astype(F32))
        return jnp.concatenate(rows, axis=0).astype(BF16)

    def packet(dom):
        return pltpu.make_async_remote_copy(
            src_ref=packets.at[pl.ds(at(dom, chunk), chunk), :],
            dst_ref=received.at[pl.ds(at(my_dom, chunk), chunk), :],
            send_sem=packet_send.at[dom], recv_sem=packet_recv.at[my_dom],
            device_id={"slab": my_slab, "dom": dom}, device_id_type=pl.DeviceIdType.MESH,
        )

    def partner(i):
        apart = lax.rem(i, 2) * (doms // 2) + lax.div(i, 2)
        if doms & (doms - 1):
            return lax.rem(my_dom + apart, doms)
        other, bit = 0, 1
        while bit < doms:
            differ = lax.rem(lax.div(my_dom, bit) + lax.div(apart, bit), 2)
            other, bit = other + differ * bit, bit * 2
        return other

    def send_packet(i, carry):
        dom = partner(i)
        packets[pl.ds(at(dom, chunk), chunk), :] = pick(dom)
        packet(dom).start()
        return carry

    lax.fori_loop(1, doms, send_packet, 0, unroll=3)
    received[pl.ds(at(my_dom, chunk), chunk), :] = pick(my_dom)

    lax.fori_loop(new_count // 32, new_count // 16, prepare_mass, 0)

    def prepare_cross(j, carry):
        pair_blocks(cross_ref, j, block)

        def cut(i, inner):
            cross[pl.ds(at(j * 8 + i, LANES), LANES), :] = jnp.transpose(
                block[pl.ds(at(i, LANES), LANES), :]
            ).astype(BF16)
            return inner

        return lax.fori_loop(0, 8, cut, carry, unroll=4)

    loads[2].wait()
    lax.fori_loop(0, slots // 16, prepare_cross, 0)

    def arrive(dom, carry):
        @pl.when(dom != my_dom)
        def _():
            pltpu.make_async_remote_copy(
                src_ref=packets.at[pl.ds(at(dom, chunk), chunk), :],
                dst_ref=received.at[pl.ds(at(dom, chunk), chunk), :],
                send_sem=packet_send.at[dom], recv_sem=packet_recv.at[dom],
                device_id={"slab": my_slab, "dom": dom}, device_id_type=pl.DeviceIdType.MESH,
            ).wait()

        return carry

    senders = 16 // cap

    def product(step, carry):
        j, h = lax.div(step, senders // 2), lax.rem(step, senders // 2)
        first = received[pl.ds(at(j * senders + h, chunk), chunk), :].astype(F32)
        second = received[pl.ds(at(j * senders + senders // 2 + h, chunk), chunk), :].astype(F32)
        for c in range(cap):
            part = slice(c * HALF, (c + 1) * HALF)
            pair = j * 8 + h * cap + c
            field = jnp.concatenate(interleave(first[part], second[part]), axis=0).astype(BF16)
            matrix = cross[pl.ds(at(pair, LANES), LANES), :]
            contrib[pl.ds(at(pair, V), V), :] = jnp.dot(
                field, matrix, preferred_element_type=F32
            )
        return carry

    own_half = jnp.where(my_dom >= doms // 2, 1, 0)
    for half in (own_half, 1 - own_half):
        lax.fori_loop(0, doms // 2, lambda n, c, half=half: arrive(half * (doms // 2) + n, c), 0)
        lax.fori_loop(0, doms // 4, lambda n, c, half=half: product(half * (doms // 4) + n, c), 0, unroll=4)

    shape = (new_count, slots)
    onehot = jnp.where(lax.broadcasted_iota(jnp.int32, shape, 0) == target_ref[...], 1.0, 0.0).astype(BF16)
    pairs_in = slots // 2

    def scatter(t, carry):
        even = contrib[pl.ds(t, pairs_in, stride=V), :]
        odd = contrib[pl.ds(HALF + t, pairs_in, stride=V), :]
        first, second = interleave(even, odd)
        rows = []
        for j in range(pairs_in // 8):
            rows += [first[j * 8:j * 8 + 8], second[j * 8:j * 8 + 8]]
        terms = jnp.concatenate(split(jnp.concatenate(rows, axis=0)), axis=1)
        total = jnp.dot(onehot, terms, preferred_element_type=F32)
        total = total[:, :LANES] + total[:, LANES:]
        for j in range(new_count // 16):
            even, odd = interleave(total[j * 16:j * 16 + 8], total[j * 16 + 8:j * 16 + 16])
            residual[pl.ds(j * 8 * V + t, 8, stride=V), :] = even
            residual[pl.ds(j * 8 * V + HALF + t, 8, stride=V), :] = odd
        return carry

    lax.fori_loop(0, HALF, scatter, 0, unroll=6)

    pairs = new_count // 2

    def apply_mass(pair, field):
        terms = jnp.concatenate(split(field), axis=0)
        result = jnp.dot(terms, blocks[pl.ds(at(pair, LANES), LANES), :], preferred_element_type=F32)
        return (result[V:, :LANES] + result[:V, LANES:]) + result[:V, :LANES]

    def sum_start(step, parts):
        stack = jnp.sum(jnp.concatenate(parts, axis=0), axis=1, keepdims=True)
        half = stack.shape[0] // 2
        own = jnp.concatenate([column_to_row(stack[:half]), column_to_row(stack[half:])], axis=0)
        sums[step] = own

        def send(i, where):
            pltpu.make_async_remote_copy(
                src_ref=sums.at[step], dst_ref=sums_in.at[step, i],
                send_sem=sum_send.at[step], recv_sem=sum_recv.at[step],
                device_id=where, device_id_type=pl.DeviceIdType.MESH,
            ).start()

        each_device(send)
        return own

    def sum_end(step, own, count):
        arrived = sums_in.at[step, 0:devices - 1]
        pltpu.make_async_copy(arrived, arrived, sum_recv.at[step]).wait()
        total = own + jnp.sum(sums_in[step, 0:devices - 1], axis=0)
        half = count * V // 2
        column = jnp.concatenate([row_to_column(total[:1], half), row_to_column(total[1:], half)], axis=0)
        return [column[n * V:(n + 1) * V] for n in range(count)]

    zero = jnp.zeros((V, LANES), F32)
    small = jnp.zeros((HALF, LANES), F32)

    def first_pass(pair, carry):
        bb, bw, ww, wq = carry
        at_pair = pl.ds(at(pair, V), V)
        b = residual[at_pair, :]
        w = apply_mass(pair, b)
        image[at_pair, :] = w
        q = apply_mass(pair, w)
        image2[at_pair, :] = q
        return bb + b * b, bw + b * w, ww + w * w, wq + w * q

    own = sum_start(0, lax.fori_loop(0, pairs, first_pass, (zero,) * 4, unroll=16))

    def third_image(pair, carry):
        at_pair = pl.ds(at(pair, V), V)
        image3[at_pair, :] = apply_mass(pair, image2[at_pair, :])
        return carry

    lax.fori_loop(0, pairs, third_image, 0, unroll=8)
    bb, bw, ww, wq = sum_end(0, own, 4)

    alpha = bb / bw
    norm = alpha * (alpha * ww) - bb
    weighted = bw - 2.0 * (alpha * ww) + alpha * (alpha * wq)
    beta = norm / bb
    curve = weighted - beta * (norm / alpha)
    sound = jnp.logical_and(norm > FLOOR * bb, curve > 0.0)
    beta = jnp.where(sound, beta, 0.0)
    alpha1 = jnp.where(sound, norm / jnp.where(sound, curve, 1.0), alpha)

    dots = []
    for part in range(2):
        rows = slice(part * HALF, (part + 1) * HALF)
        a0, a1, grow = (
            jnp.broadcast_to(value[rows], (HALF, LANES)) for value in (alpha, alpha1, 1.0 + beta)
        )

        def second_pass(pair, carry, part=part, a0=a0, a1=a1, grow=grow):
            rr, rw, rs, ps, rp = carry
            at_pair = pl.ds(at(pair * 2 + part, HALF), HALF)
            b, w, q, t = (ref[at_pair, :] for ref in (residual, image, image2, image3))
            p = grow * b - a0 * w
            s = grow * w - a0 * q
            r = (b - a0 * w) - a1 * s
            v = (w - a0 * q) - a1 * (grow * q - a0 * t)
            image3[at_pair, :] = a0 * b + a1 * p
            image2[at_pair, :] = p
            residual[at_pair, :] = r
            return rr + r * r, rw + r * v, rs + r * s, ps + p * s, rp + r * p

        dots.append(lax.fori_loop(0, pairs, second_pass, (small,) * 5, unroll=4))

    own = sum_start(1, [half for pair in zip(*dots) for half in pair])

    def flatten(pair, carry):
        at_pair = pl.ds(at(pair, V), V)
        number = lax.div(pair, 8) * 16 + lax.rem(pair, 8)
        for src, dst in ((image3, flat_x), (image2, flat_p), (residual, flat_r)):
            value = src[at_pair, :]
            first, second = interleave(value[:HALF], value[HALF:])
            dst[pl.ds(at(number, HALF), HALF), :] = first
            dst[pl.ds(at(number + 8, HALF), HALF), :] = second
        return carry

    lax.fori_loop(0, pairs, flatten, 0, unroll=4)
    rr, rw, rs, ps, rp = sum_end(1, own, 5)
    beta = -rs / ps
    alpha = (rr + beta * rp) / (rw + beta * (2.0 * rs + beta * ps))

    def flat_factor(column):
        wide = jnp.broadcast_to(column, (V, LANES))
        return jnp.where(left_half((HALF, LANES)), wide[:HALF], wide[HALF:])

    factor_r = flat_factor(alpha)
    factor_p = flat_factor(alpha * beta)

    used = group * HALF

    def code(dom):
        rows = []
        for g in range(group):
            which = pl.ds(order_ref[0, dom * group + g] * HALF, HALF)
            rows.append(flat_x[which, :] + (factor_p * flat_p[which, :] + factor_r * flat_r[which, :]))
        value = jnp.concatenate(rows, axis=0)
        top = jnp.maximum(jnp.max(jnp.abs(value), axis=1, keepdims=True), 1e-30)
        coded = jnp.round(value * (LIMIT / top)).astype(jnp.int32)
        if code_rows > used:
            coded = jnp.concatenate([coded, jnp.zeros((code_rows - used, LANES), jnp.int32)], axis=0)
        return coded.astype(jnp.int16), column_to_row(top * (1.0 / LIMIT))

    def code_copies(to, frm, dst):
        where = {"slab": my_slab, "dom": to}
        return [
            pltpu.make_async_remote_copy(
                src_ref=codes.at[pl.ds(at(to, code_rows), code_rows), :],
                dst_ref=codes_in.at[pl.ds(at(dst, code_rows), code_rows), :],
                send_sem=code_send.at[to], recv_sem=code_recv.at[frm],
                device_id=where, device_id_type=pl.DeviceIdType.MESH,
            ),
            pltpu.make_async_remote_copy(
                src_ref=scales.at[pl.ds(to, 1), :], dst_ref=scales_in.at[pl.ds(dst, 1), :],
                send_sem=scale_send.at[to], recv_sem=scale_recv.at[frm],
                device_id=where, device_id_type=pl.DeviceIdType.MESH,
            ),
        ]

    def send_code(i, carry):
        dom = partner(i)
        coded, scale = code(dom)
        codes[pl.ds(at(dom, code_rows), code_rows), :] = coded
        scales[pl.ds(dom, 1), :] = scale
        for copy in code_copies(dom, my_dom, my_dom):
            copy.start()
        return carry

    lax.fori_loop(1, doms, send_code, 0, unroll=3)
    coded, scale = code(my_dom)

    codes_out[pl.ds(at(my_dom, code_rows), code_rows), :] = coded
    scales_out[pl.ds(my_dom, 1), :] = scale

    def take(dom, carry):
        @pl.when(dom != my_dom)
        def _():
            for copy in code_copies(dom, dom, dom):
                copy.wait()
            here = pl.ds(at(dom, code_rows), code_rows)
            codes_out[here, :] = codes_in[here, :]
            scales_out[pl.ds(dom, 1), :] = scales_in[pl.ds(dom, 1), :]

        return carry

    lax.fori_loop(0, doms, take, 0)

    for step in range(SUMS):
        left = sums_in.at[step, 0:devices - 1]
        pltpu.make_async_copy(left, left, sum_send.at[step]).wait()

    @pl.when(my_slab < slabs - 1)
    def _():
        up.wait_send()

    @pl.when(my_slab > 0)
    def _():
        down.wait_send()


def unfold_kernel(used, code_rows, codes_ref, scales_ref, dst, placed, held, store_sem):
    senders = 8 * HALF // used
    stores = []
    for block in range(held.shape[0] // 8):
        for n in range(senders):
            dom = block * senders + n
            value = codes_ref[dom * code_rows:(dom + 1) * code_rows, :].astype(jnp.int32).astype(F32)[:used]
            scale = row_to_column(scales_ref[dom:dom + 1, :], used)
            row = (block * senders + n) * used
            placed[row:row + used, :] = value * scale
        part = slice(block * 8, (block + 1) * 8)
        for t in range(HALF):
            held[part, t * LANES:(t + 1) * LANES] = placed[pl.ds(block * 8 * HALF + t, 8, stride=HALF), :]
        store = pltpu.make_async_copy(held.at[part, :], dst.at[part, :], store_sem.at[block])
        store.start()
        stores.append(store)
    for store in stores:
        store.wait()


def unfold(codes, scales, new_count, used, code_rows):
    shape = (new_count, V * Q)
    return pl.pallas_call(
        functools.partial(unfold_kernel, used, code_rows),
        out_shape=jax.ShapeDtypeStruct(shape, F32),
        in_specs=[pl.BlockSpec(memory_space=pltpu.VMEM)] * 2,
        out_specs=pl.BlockSpec(memory_space=pl.ANY),
        scratch_shapes=[
            pltpu.VMEM((new_count * HALF, LANES), F32),
            pltpu.VMEM(shape, F32),
            pltpu.SemaphoreType.DMA((new_count // 8,)),
        ],
        compiler_params=pltpu.CompilerParams(vmem_limit_bytes=56 * 1024 * 1024),
    )(codes, scales)


def per_device(slabs, doms, state, send_index, send_count, slot_target, cross_mass, mass, new_order):
    cap = send_index.shape[3]
    new_count = mass.shape[1]
    group = new_count // doms
    slots = doms * cap
    pool_rows = (state.shape[1] + 2 * RIM) * HALF
    rim_rows = RIM * HALF
    code_rows = -(-group * HALF // 16) * 16
    devices = slabs * doms
    steps = SUMS
    vmem, smem = pltpu.VMEM, pltpu.SMEM
    dma = pltpu.SemaphoreType.DMA
    field = vmem((new_count * HALF, LANES), F32)
    scratch = [
        vmem(state.shape[1:], BF16),
        vmem((slots, Q * Q), BF16),
        vmem((new_count, Q * Q), F32),
        dma((3,)),
        vmem((pool_rows, LANES), F32),
        *[vmem((rim_rows, LANES), BF16)] * 4,
        vmem((slots * HALF, LANES), BF16),
        vmem((slots * HALF, LANES), BF16),
        vmem((8 * LANES, LANES), F32),
        vmem((slots // 2 * LANES, LANES), BF16),
        vmem((new_count // 2 * LANES, 2 * LANES), BF16),
        vmem((slots * HALF, LANES), F32),
        *[field] * 7,
        vmem((doms * code_rows, LANES), jnp.int16),
        vmem((doms * code_rows, LANES), jnp.int16),
        vmem((doms, LANES), F32),
        vmem((doms, LANES), F32),
        vmem((steps, 2, LANES), F32),
        vmem((steps, devices, 2, LANES), F32),
        dma((2,)), dma((2,)), dma((doms,)), dma((doms,)),
        dma((steps,)), dma((steps,)),
        dma((doms,)), dma((doms,)), dma((doms,)), dma((doms,)),
    ]
    codes, scales = pl.pallas_call(
        functools.partial(kernel, slabs, doms, cap, group),
        out_shape=(
            jax.ShapeDtypeStruct((doms * code_rows, LANES), jnp.int16),
            jax.ShapeDtypeStruct((doms, LANES), F32),
        ),
        in_specs=[pl.BlockSpec(memory_space=smem)] * 3 + [pl.BlockSpec(memory_space=vmem)]
        + [pl.BlockSpec(memory_space=pltpu.HBM)] * 3,
        out_specs=[pl.BlockSpec(memory_space=vmem)] * 2,
        scratch_shapes=scratch,
        compiler_params=pltpu.CompilerParams(
            collective_id=0, has_side_effects=True, vmem_limit_bytes=56 * 1024 * 1024
        ),
        cost_estimate=pl.CostEstimate(flops=10**9, bytes_accessed=4 * 10**6, transcendentals=0),
    )(
        send_index[0, 0].T, send_count[0], new_order[0], slot_target[0],
        state[0], cross_mass[0, 0], mass[0],
    )
    return unfold(codes, scales, new_count, group * HALF, code_rows)[None]


def solution(mesh):
    in_specs = (
        P("dom", "slab", None),
        P("dom", "slab", None, None),
        P("dom", "slab", None),
        P("dom", "slab", None),
        P("dom", "slab", None, None),
        P("dom", "slab", None),
        P("dom", "slab", None),
    )
    return jax.shard_map(
        functools.partial(per_device, mesh.shape["slab"], mesh.shape["dom"]),
        mesh=mesh, in_specs=in_specs, out_specs=P("dom", "slab", None), check_vma=False,
    )
```
